128 devices in a mesh: ctx: 32 (over x, z_lo, y), head: 4 (over z_hi, core).
Axes of the slice: x: 4, y: 4, z: 4 (z_hi: 2, z_lo: 2; z = z_hi * 2 + z_lo), core: 2. Of those that a mesh axis runs over, the one named last changes fastest.
Arguments:
- raw_values: bfloat16 [8192, 16384], P('ctx', 'head'), may hold values from -3 to 3
- state_ports: bfloat16 [8192, 2, 2048], P('ctx', None, 'head'), may hold values from -0.75 to 0.75
- step_raw: float32 [8192, 256], P('ctx', 'head')
- decay_log: float32 [256], P('head')
- skip_gain: float32 [256], P('head'), may hold values from 0.5 to 1.5
- conv_values: bfloat16 [4, 16384], P(None, 'head'), may hold values from -3 to 3
- conv_ports: bfloat16 [4, 2, 2048], P(None, None, 'head'), may hold values from -3 to 3
- prompt_slot: int32 [32], P('ctx'), may hold values from 0 to 1
- row_slot: int32 [256], P('ctx'), may hold values from 0 to 1, as said below
- cache_states: bfloat16 [64, 256, 64, 256], P('ctx', 'head'), may hold values from -6 to 6
- cache_values: bfloat16 [64, 3, 16384], P('ctx', None, 'head'), may hold values from -3 to 3
- cache_ports: bfloat16 [64, 3, 2, 2048], P('ctx', None, None, 'head'), may hold values from -0.75 to 0.75
- new_values: bfloat16 [4, 256, 16384], P(None, 'ctx', 'head'), may hold values from -3 to 3
- new_ports: bfloat16 [4, 256, 2, 2048], P(None, 'ctx', None, 'head'), may hold values from -0.75 to 0.75
- new_steps: float32 [4, 256, 256], P(None, 'ctx', 'head'), may hold values from -2 to 60
- out_weight: bfloat16 [16384, 8192], P('head', 'ctx'), may hold values from -0.046875 to 0.046875
Outputs:
- scan_out: bfloat16 [8192, 16384], P('ctx', 'head')
- decoded_out: bfloat16 [4, 256, 8192], P(None, 'head', 'ctx')
The draws below stay inside these ranges and needn't reach their ends.
Inputs may be any that keep to these rules, and one draw needn't show every extreme that they name: `row_slot`: every slot of a group is read by one or more of the group's 8 rows.
All inputs are finite; a program needn't handle non-finite values.
Results may differ from the reference program's by a relative error of at most 0.013.
Values may be sent and summed in bfloat16 or wider, within the bound.
No kernel may reach another device: no remote copies, remote signals or barrier semaphores. Data moves between devices by JAX's collectives and lax.ppermute only.
A program may use at most 320 MiB of HBM per device.

```python
import math
import jax
import jax.numpy as jnp
from jax import lax

D = 8192
HEADS = 256
P_SIZE = 64
N = 256
G = 8
CONV = 4
SPAN = 256
SLOTS = 2
DROWS = 8
STEPS = 4
TOKENS = 8192
DGROUPS = 32
ROWS = 256
CACHE_ROWS = 64


def slow_heads(key, share):
    return jax.random.uniform(key, (HEADS,)) < share


def slow_base():
    return 250.0 * math.sqrt(TOKENS / N) / TOKENS


def fast_base():
    return 80.0 / math.sqrt(N)


def centred_draw(key, shape, scale, bound):
    return jnp.clip(scale * jax.random.normal(key, shape), -bound, bound)


def draw_raw_values(key, part):
    key = jax.random.fold_in(key, 31)
    return centred_draw(key, (TOKENS, HEADS * P_SIZE), 0.5, 3.0).astype(jnp.bfloat16)


def draw_state_ports(key, part):
    key = jax.random.fold_in(key, 37)
    return centred_draw(key, (TOKENS, 2, G * N), 0.125, 0.75).astype(jnp.bfloat16)


def draw_decay_log(key, part):
    share = 0.5
    slow = slow_heads(key, share)
    key = jax.random.fold_in(key, 5)
    first, second = jax.random.split(key)
    ratio = jnp.exp(jax.random.uniform(first, (HEADS,), minval=math.log(0.2), maxval=math.log(1.0)))
    memory = jax.random.uniform(second, (HEADS,), minval=50.0, maxval=85.0)
    rate = jnp.where(slow, ratio / (slow_base() * TOKENS), 1.0 / (fast_base() * memory))
    return jnp.log(rate).astype(jnp.float32)


def draw_step_raw(key, part):
    share = 0.5
    slow = slow_heads(key, share)
    key = jax.random.fold_in(key, 7)
    first, second = jax.random.split(key)
    blocks = TOKENS // SPAN
    offsets = jax.random.uniform(first, (blocks, 1, HEADS), minval=-1.2, maxval=1.2)
    noise = 0.8 * jax.random.normal(second, (blocks, SPAN, HEADS))
    base = jnp.where(slow, slow_base(), fast_base())
    sizes = base[None, None, :] * jnp.exp(offsets + noise)
    inverse = sizes + jnp.log(-jnp.expm1(-sizes))
    return inverse.reshape(TOKENS, HEADS).astype(jnp.float32)


def draw_row_slot(key, part):
    key = jax.random.fold_in(key, 21)
    group_keys = jax.random.split(key, ROWS // DROWS)

    def one_group(group_key):
        first, second = jax.random.split(group_key)
        extra = jax.random.randint(first, (DROWS - SLOTS,), 0, SLOTS).astype(jnp.int32)
        every = jnp.concatenate([jnp.arange(SLOTS, dtype=jnp.int32), extra])
        return jax.random.permutation(second, every)
    return jax.vmap(one_group)(group_keys).reshape(ROWS).astype(jnp.int32)


def with_ends(drawn, key, least, high):
    longest = drawn.shape.index(max(drawn.shape))
    spots = []
    for shift in (0, 1):
        where = [jax.random.randint(jax.random.fold_in(key, axis), (), 0, length) for axis, length in enumerate(drawn.shape)]
        where[longest] = (where[longest] + shift) % drawn.shape[longest]
        spots.append(tuple(where))
    return drawn.at[spots[0]].set(least).at[spots[1]].set(high)


def block_levels(key, extent, cuts, low, top_value):
    loudness, own = 1.0, jax.random.fold_in(key, 6)
    for axis_at, parts in cuts:
        heights = jnp.exp(jax.random.uniform(jax.random.fold_in(own, axis_at), (parts,), jnp.float32, low / len(cuts), top_value / len(cuts)))
        loudness = loudness * jnp.repeat(heights, extent[axis_at] // parts).reshape([-1 if axis == axis_at else 1 for axis in range(len(extent))])
    return loudness


def scatter_about(key, shape, deviation, most, pieces=(), held_as=jnp.bfloat16):
    values = deviation * jax.random.normal(key, shape, jnp.float32)
    if pieces:
        values = values * block_levels(key, shape, pieces, -0.22, 0.18)
    return jnp.clip(values, -most, most).astype(held_as)


def setup_inputs(seed: int = 0) -> dict:
    key_of = jax.random.split(jax.random.key(seed), 17)
    raw_values = draw_raw_values(jax.random.fold_in(key_of[16], 71), 0)
    state_ports = draw_state_ports(jax.random.fold_in(key_of[16], 71), 0)
    step_raw = draw_step_raw(jax.random.fold_in(key_of[16], 71), 0)
    decay_log = draw_decay_log(jax.random.fold_in(key_of[16], 71), 0)
    skip_gain = jnp.clip(0.5 + 1.0 * jax.random.uniform(key_of[4], (HEADS,), jnp.float32) ** block_levels(key_of[4], (HEADS,), ((0, 4),), -0.2, 0.2), 0.5, 1.5)
    conv_values = scatter_about(key_of[5], (CONV, HEADS * P_SIZE), CONV ** -0.5, 3.0, ((1, 4),))
    conv_ports = scatter_about(key_of[6], (CONV, 2, G * N), CONV ** -0.5, 3.0, ((2, 4),))
    prompt_slot = with_ends(jax.random.randint(key_of[7], (DGROUPS,), 0, SLOTS), jax.random.fold_in(key_of[7], 1), 0, SLOTS - 1).astype(jnp.int32)
    row_slot = draw_row_slot(jax.random.fold_in(key_of[16], 71), 0)
    cache_states = scatter_about(key_of[9], (CACHE_ROWS, HEADS, P_SIZE, N), 1.0, 6.0, ((0, 32), (1, 4)))
    cache_values = scatter_about(key_of[10], (CACHE_ROWS, CONV - 1, HEADS * P_SIZE), 0.5, 3.0, ((0, 32), (2, 4)))
    cache_ports = scatter_about(key_of[11], (CACHE_ROWS, CONV - 1, 2, G * N), 0.125, 0.75, ((0, 32), (3, 4)))
    new_values = scatter_about(key_of[12], (STEPS, ROWS, HEADS * P_SIZE), 0.5, 3.0, ((1, 32), (2, 4)))
    new_ports = scatter_about(key_of[13], (STEPS, ROWS, 2, G * N), 0.125, 0.75, ((1, 32), (3, 4)))
    new_steps = jnp.clip(-2.0 + 62.0 * jax.random.uniform(key_of[14], (STEPS, ROWS, HEADS), jnp.float32) ** block_levels(key_of[14], (STEPS, ROWS, HEADS), ((1, 32), (2, 4)), -0.2, 0.2), -2.0, 60.0)
    out_weight = scatter_about(key_of[15], (HEADS * P_SIZE, D), (HEADS * P_SIZE) ** -0.5, 0.046875, ((0, 4), (1, 32)))
    return {"raw_values": raw_values, "state_ports": state_ports, "step_raw": step_raw, "decay_log": decay_log, "skip_gain": skip_gain, "conv_values": conv_values, "conv_ports": conv_ports, "prompt_slot": prompt_slot, "row_slot": row_slot, "cache_states": cache_states, "cache_values": cache_values, "cache_ports": cache_ports, "new_values": new_values, "new_ports": new_ports, "new_steps": new_steps, "out_weight": out_weight}


def window_mix(windows, weights):
    mixture = weights[0].astype(jnp.float32) * windows[0].astype(jnp.float32)
    for position in range(1, len(windows)):
        mixture = mixture + weights[position].astype(jnp.float32) * windows[position].astype(jnp.float32)
    return jax.nn.silu(mixture).astype(jnp.bfloat16)


def causal_mix(raw_rows, weights):
    length = raw_rows.shape[0]
    padded = jnp.concatenate([jnp.zeros((CONV - 1,) + raw_rows.shape[1:], raw_rows.dtype), raw_rows], axis=0)
    return window_mix([padded[position:position + length] for position in range(CONV)], weights)


def span_pass(carry_state, inputs, decay_rate, skip_heads):
    values, write_rows, read_rows, step_sizes = inputs
    running = jnp.cumsum(step_sizes * decay_rate[None, :], axis=0)
    scores = jnp.dot(read_rows, write_rows.T, preferred_element_type=jnp.float32)
    causal = jnp.arange(SPAN)[:, None] >= jnp.arange(SPAN)[None, :]
    across = running.T
    log_gaps = across[:, :, None] - across[:, None, :]
    decays = jnp.where(causal[None], jnp.exp(jnp.where(causal[None], log_gaps, 0.0)), 0.0)
    weights = (scores[None] * decays * step_sizes.T[:, None, :]).astype(jnp.bfloat16)
    within = jnp.einsum('hts,shp->thp', weights.astype(jnp.float32), values.astype(jnp.float32))
    carried = jnp.exp(running)[:, :, None] * jnp.einsum('tn,hpn->thp', read_rows.astype(jnp.float32), carry_state, precision=lax.Precision.HIGHEST)
    outputs = (within + carried + skip_heads[None, :, None] * values.astype(jnp.float32)).astype(jnp.bfloat16)
    ending = running[-1]
    scaled = (values.astype(jnp.float32) * (step_sizes * jnp.exp(ending[None, :] - running))[:, :, None]).astype(jnp.bfloat16)
    fresh_state = jnp.einsum('shp,sn->hpn', scaled.astype(jnp.float32), write_rows.astype(jnp.float32))
    return jnp.exp(ending)[:, None, None] * carry_state + fresh_state, outputs


def reference(raw_values, state_ports, step_raw, decay_log, skip_gain, conv_values, conv_ports, prompt_slot, row_slot, cache_states, cache_values, cache_ports, new_values, new_ports, new_steps, out_weight):
    per_group = HEADS // G
    group_width = per_group * P_SIZE
    blocks = TOKENS // SPAN
    port_mix = causal_mix(state_ports, conv_ports)
    write_all = port_mix[:, 0].reshape(TOKENS, G, N)
    read_all = port_mix[:, 1].reshape(TOKENS, G, N)
    step_sizes = jax.nn.softplus(step_raw)
    decay_rate = -jnp.exp(decay_log)

    def one_group(group_index):
        raw_slice = lax.dynamic_slice_in_dim(raw_values, group_index * group_width, group_width, 1)
        tap_slice = lax.dynamic_slice_in_dim(conv_values, group_index * group_width, group_width, 1)
        value_mix = causal_mix(raw_slice, tap_slice).reshape(blocks, SPAN, per_group, P_SIZE)
        write_rows = lax.dynamic_index_in_dim(write_all, group_index, 1, keepdims=False).reshape(blocks, SPAN, N)
        read_rows = lax.dynamic_index_in_dim(read_all, group_index, 1, keepdims=False).reshape(blocks, SPAN, N)
        group_steps = lax.dynamic_slice_in_dim(step_sizes, group_index * per_group, per_group, 1).reshape(blocks, SPAN, per_group)
        group_rates = lax.dynamic_slice_in_dim(decay_rate, group_index * per_group, per_group, 0)
        group_gains = lax.dynamic_slice_in_dim(skip_gain, group_index * per_group, per_group, 0)

        def advance(carry_state, inputs):
            return span_pass(carry_state, inputs, group_rates, group_gains)

        final_group, outputs = lax.scan(advance, jnp.zeros((per_group, P_SIZE, N), jnp.float32), (value_mix, write_rows, read_rows, group_steps))
        return outputs.reshape(TOKENS, group_width), final_group

    group_outputs, finals = lax.map(one_group, jnp.arange(G, dtype=jnp.int32))
    scan_out = group_outputs.transpose(1, 0, 2).reshape(TOKENS, HEADS * P_SIZE)
    final_state = finals.reshape(HEADS, P_SIZE, N).astype(jnp.bfloat16)
    tail_values = raw_values[TOKENS - CONV + 1:]
    tail_ports = state_ports[TOKENS - CONV + 1:]
    rates_grouped = decay_rate.reshape(G, per_group)
    gains_grouped = skip_gain.reshape(G, per_group)

    def one_row(row_index):
        group_number = row_index // DROWS
        cache_row = group_number * SLOTS + row_slot[row_index]
        chosen = row_slot[row_index] == prompt_slot[group_number]
        carry_state = jnp.where(chosen, final_state, cache_states[cache_row]).astype(jnp.float32).reshape(G, per_group, P_SIZE, N)
        conv_rows = jnp.where(chosen, tail_values, cache_values[cache_row])
        conv_pairs = jnp.where(chosen, tail_ports, cache_ports[cache_row])
        results = []
        for step_index in range(STEPS):
            window_values = jnp.concatenate([conv_rows, new_values[step_index, row_index][None]], axis=0)
            window_ports = jnp.concatenate([conv_pairs, new_ports[step_index, row_index][None]], axis=0)
            value_now = window_mix([window_values[position] for position in range(CONV)], conv_values)
            ports_now = window_mix([window_ports[position] for position in range(CONV)], conv_ports)
            write_now = ports_now[0].reshape(G, N).astype(jnp.float32)
            read_now = ports_now[1].reshape(G, N).astype(jnp.float32)
            size_now = jax.nn.softplus(new_steps[step_index, row_index]).reshape(G, per_group)
            decay_now = jnp.exp(size_now * rates_grouped)
            value_heads = value_now.astype(jnp.float32).reshape(G, per_group, P_SIZE)
            carry_state = decay_now[:, :, None, None] * carry_state + (size_now[:, :, None] * value_heads)[..., None] * write_now[:, None, None, :]
            readout = jnp.einsum('gjpn,gn->gjp', carry_state, read_now, precision=lax.Precision.HIGHEST)
            results.append((readout + gains_grouped[:, :, None] * value_heads).astype(jnp.bfloat16).reshape(HEADS * P_SIZE))
            conv_rows = window_values[1:]
            conv_pairs = window_ports[1:]
        return jnp.stack(results)

    decoded = lax.map(one_row, jnp.arange(ROWS, dtype=jnp.int32))
    flat_rows = decoded.transpose(1, 0, 2).reshape(STEPS * ROWS, HEADS * P_SIZE)
    decoded_out = jnp.dot(flat_rows, out_weight, preferred_element_type=jnp.float32).astype(jnp.bfloat16).reshape(STEPS, ROWS, D)
    return scan_out, decoded_out
```

```python
import functools

import jax
import jax.numpy as jnp
from jax import lax
from jax.experimental import pallas as pl
from jax.experimental.pallas import tpu as pltpu
from jax.sharding import PartitionSpec as P

P_SIZE = 64
N = 256
CONV = 4
SPAN = 256
X, Z, Y = 4, 2, 4
F32 = jnp.float32
BF16 = jnp.bfloat16
SMEM = pl.BlockSpec(memory_space=pltpu.SMEM)
VMEM = pl.BlockSpec(memory_space=pltpu.VMEM)
VMEM_BYTES = 48 * 2**20


def place(x, z, y):
    return (x % X * Z + z % Z) * Y + y % Y


def shifted(value, dx=0, dz=0, dy=0):
    pairs = [
        (place(x, z, y), place(x + dx, z + dz, y + dy))
        for x in range(X)
        for z in range(Z)
        for y in range(Y)
    ]
    return lax.ppermute(value, "ctx", pairs)


def call(kernel, out_shape, scratch=(), n_in=None, us=2.0, grid_spec=None, aliases=None):
    params = dict(
        out_shape=out_shape,
        compiler_params=pltpu.CompilerParams(vmem_limit_bytes=VMEM_BYTES),
        cost_estimate=pl.CostEstimate(
            flops=int(us * 1.0e9), bytes_accessed=int(us * 1.0e6), transcendentals=0
        ),
    )
    if grid_spec is not None:
        return pl.pallas_call(kernel, grid_spec=grid_spec, **params)
    outs = jax.tree.map(lambda _: VMEM, out_shape)
    return pl.pallas_call(
        kernel,
        in_specs=[SMEM] + [VMEM] * (n_in - 1),
        out_specs=outs,
        scratch_shapes=list(scratch),
        **params,
    )


def sds(shape, dtype):
    return jax.ShapeDtypeStruct(shape, dtype)


def silu(value):
    return value * (0.5 + 0.5 * jnp.tanh(0.5 * value))


def softplus(value):
    return jnp.maximum(value, 0.0) + jnp.log1p(jnp.exp(-jnp.abs(value)))


def halves(value):
    high = value.astype(BF16)
    return high, (value - high.astype(F32)).astype(BF16)


def paired(value):
    high, low = halves(value)
    return jnp.concatenate([high.astype(F32), low.astype(F32)], axis=1).astype(BF16)


def head_spread(quarter, heads, width):
    row = lax.broadcasted_iota(jnp.int32, (2 * heads, width), 0)
    col = lax.broadcasted_iota(jnp.int32, (2 * heads, width), 1)
    first = quarter * (width // P_SIZE)
    match = lax.rem(row, heads) == first + lax.div(col, P_SIZE)
    return jnp.where(match, 1.0, 0.0).astype(BF16)


def dot(a, b):
    return jnp.dot(a, b, preferred_element_type=F32)


def dot_nt(a, b):
    return lax.dot_general(a, b, (((1,), (1,)), ((), ())), preferred_element_type=F32)


def ports_kernel(
    ids, ports, rim, taps, steps, steps_t, log_row, log_col,
    read_out, write_t_out, run_out, row_out, factor_out, grow_out, scr,
):
    width = ports.shape[1]
    base = rim.shape[1] - width
    scr[0:8] = rim[:, base:]
    scr[8 : 8 + SPAN] = ports[...].astype(F32)
    half = width // 2
    for part in range(2):
        lanes = slice(part * half, (part + 1) * half)
        mixture = taps[0:1, base + part * half : base + (part + 1) * half] * scr[5 : 5 + SPAN, lanes]
        for position in range(1, CONV):
            mixture = mixture + taps[
                position : position + 1, base + part * half : base + (part + 1) * half
            ] * scr[5 + position : 5 + position + SPAN, lanes]
        mixed = silu(mixture)
        if part == 0:
            write_t_out[...] = mixed.astype(BF16).astype(F32).T.astype(BF16)
        else:
            read_out[...] = mixed.astype(BF16)
    rows = lax.broadcasted_iota(jnp.int32, (SPAN, SPAN), 0)
    cols = lax.broadcasted_iota(jnp.int32, (SPAN, SPAN), 1)
    lower = jnp.where(rows >= cols, 1.0, 0.0)
    upper = jnp.where(rows <= cols, 1.0, 0.0)
    size = softplus(steps[...])
    run = jnp.dot(
        lower, size * -jnp.exp(log_row[...]), precision=lax.Precision.HIGHEST,
        preferred_element_type=F32,
    )
    size_t = softplus(steps_t[...])
    run_t = jnp.dot(
        size_t * -jnp.exp(log_col[...]), upper, precision=lax.Precision.HIGHEST,
        preferred_element_type=F32,
    )
    heads = run.shape[1]
    quarter = heads // Y
    for index in range(Y):
        run_out[index] = run[:, index * quarter : (index + 1) * quarter]
    row_out[...] = run_t - jnp.log(size_t)
    ending = run[SPAN - 1 : SPAN]
    factor_out[0:SPAN] = paired(size * jnp.exp(ending - run))
    factor_out[SPAN : SPAN + 16] = paired(jnp.broadcast_to(jnp.exp(ending), (16, heads)))
    grow_out[...] = paired(jnp.exp(run))


def state_kernel(ids, raw, rim, taps, factor, write_t, payload, mixed_out, scr, wide, scaled):
    width = raw.shape[1]
    shift = ids[0]
    scr[0:8] = rim[...]
    scr[8 : 8 + SPAN] = raw[...].astype(F32)
    spread = head_spread(shift, factor.shape[1] // 2, width)
    wide[...] = dot(factor[...], spread)
    rows = 32
    for start in range(0, SPAN, rows):
        mixture = taps[0:1] * scr[start + 5 : start + 5 + rows]
        for position in range(1, CONV):
            at = start + 5 + position
            mixture = mixture + taps[position : position + 1] * scr[at : at + rows]
        mixed = silu(mixture).astype(BF16)
        mixed_out[start : start + rows] = mixed
        scaled[start : start + rows] = (mixed.astype(F32) * wide[start : start + rows]).astype(BF16)
    for start in range(0, width, 256):
        payload[0:N, start : start + 256] = dot(
            write_t[...], scaled[:, start : start + 256]
        ).astype(BF16)
    decay = wide[SPAN : SPAN + 16]
    high = decay.astype(BF16).astype(F32)
    at = lax.broadcasted_iota(jnp.int32, decay.shape, 0)
    tail = jnp.where(at == 0, high, jnp.where(at == 1, decay - high, 0.0))
    payload[N : N + 16] = tail.astype(BF16)


def state_call(quarter, raw, rim, taps, factor, write_t):
    width_dev = raw.shape[1]
    width = width_dev // Y
    per_group = write_t.shape[0] // N
    per = Y // per_group
    grid_spec = pltpu.PrefetchScalarGridSpec(
        num_scalar_prefetch=1,
        grid=(1,),
        in_specs=[
            pl.BlockSpec((SPAN, width), lambda i, s: (0, s[0])),
            pl.BlockSpec((8, width), lambda i, s: (0, s[0])),
            pl.BlockSpec((CONV, width), lambda i, s: (0, s[0])),
            pl.BlockSpec(factor.shape, lambda i, s: (0, 0)),
            pl.BlockSpec((N, SPAN), lambda i, s: (lax.div(s[0], per), 0)),
        ],
        out_specs=[
            pl.BlockSpec((N + 16, width), lambda i, s: (0, 0)),
            pl.BlockSpec((SPAN, width), lambda i, s: (0, 0)),
        ],
        scratch_shapes=[
            pltpu.VMEM((SPAN + 8, width), F32),
            pltpu.VMEM((SPAN + 16, width), F32),
            pltpu.VMEM((SPAN, width), BF16),
        ],
    )
    return call(
        state_kernel,
        (sds((N + 16, width), BF16), sds((SPAN, width), BF16)),
        grid_spec=grid_spec,
        us=3.0,
    )(quarter, raw, rim, taps, factor, write_t)


def within_kernel(ids, read, write_t, run, row, mixed, skip, out, scores):
    scores[...] = dot(read[...], write_t[...])
    half = SPAN // 2
    rows = lax.broadcasted_iota(jnp.int32, (half, half), 0)
    cols = lax.broadcasted_iota(jnp.int32, (half, half), 1)
    causal = rows >= cols
    left = lax.broadcasted_iota(jnp.int32, (half, 2 * P_SIZE), 1) < P_SIZE
    for pair in range(mixed.shape[1] // (2 * P_SIZE)):
        lanes = slice(pair * 2 * P_SIZE, (pair + 1) * 2 * P_SIZE)
        upper, lower = mixed[0:half, lanes], mixed[half:SPAN, lanes]
        tops, bottoms = [], []
        for member in range(2):
            head = 2 * pair + member
            col = run[0, :, head : head + 1]
            line = row[head : head + 1, :]
            w00 = jnp.where(
                causal, scores[0:half, 0:half] * jnp.exp(col[0:half] - line[:, 0:half]), 0.0
            ).astype(BF16)
            w10 = (scores[half:SPAN, 0:half] * jnp.exp(col[half:SPAN] - line[:, 0:half])).astype(BF16)
            w11 = jnp.where(
                causal,
                scores[half:SPAN, half:SPAN] * jnp.exp(col[half:SPAN] - line[:, half:SPAN]),
                0.0,
            ).astype(BF16)
            tops.append(dot(w00, upper))
            bottoms.append(dot(w10, upper) + dot(w11, lower))
        gain = skip[0:1, lanes]
        out[0:half, lanes] = jnp.where(left, tops[0], tops[1]) + gain * upper.astype(F32)
        out[half:SPAN, lanes] = jnp.where(left, bottoms[0], bottoms[1]) + gain * lower.astype(F32)


def within_call(quarter, read, write_t, run, row, mixed, skip):
    width = mixed.shape[1]
    per = Y // (write_t.shape[0] // N)
    heads = width // P_SIZE
    grid_spec = pltpu.PrefetchScalarGridSpec(
        num_scalar_prefetch=1,
        grid=(1,),
        in_specs=[
            pl.BlockSpec((SPAN, N), lambda i, s: (0, lax.div(s[0], per))),
            pl.BlockSpec((N, SPAN), lambda i, s: (lax.div(s[0], per), 0)),
            pl.BlockSpec((1, SPAN, heads), lambda i, s: (s[0], 0, 0)),
            pl.BlockSpec((heads, SPAN), lambda i, s: (s[0], 0)),
            pl.BlockSpec((SPAN, width), lambda i, s: (0, 0)),
            pl.BlockSpec((1, width), lambda i, s: (0, s[0])),
        ],
        out_specs=pl.BlockSpec((SPAN, width), lambda i, s: (0, 0)),
        scratch_shapes=[pltpu.VMEM((SPAN, SPAN), F32)],
    )
    return call(within_kernel, sds((SPAN, width), F32), grid_spec=grid_spec, us=4.0)(
        quarter, read, write_t, run, row, mixed, skip
    )


def carried_kernel(ids, grow, read, *refs):
    withins, states, out = refs[0:Y], refs[Y : 2 * Y], refs[2 * Y]
    width = withins[0].shape[1]
    groups = read.shape[1] // N
    per = Y // groups
    for index in range(Y):
        quarter = lax.rem(ids[2] + index, Y)
        group = lax.div(quarter, per)
        spread = head_spread(quarter, grow.shape[1] // 2, width)
        reads = read[:, pl.ds(pl.multiple_of(group * N, N), N)]
        for start in range(0, width, 256):
            lanes = slice(start, start + 256)
            carried = dot(grow[...], spread[:, lanes]) * dot(reads, states[index][:, lanes])
            out[:, pl.ds(pl.multiple_of(quarter * width + start, 256), 256)] = (
                withins[index][:, lanes] + carried
            ).astype(BF16)


def decay_row(payload):
    tail = payload[N : N + 16].astype(F32)
    return tail[0:1] + tail[1:2]


def row_total_kernel(ids, *refs):
    states, out = refs[0:Y], refs[Y]
    spots = [lax.rem(ids[2] + index, Y) for index in range(Y)]
    decays = [decay_row(state) for state in states]
    width = states[0].shape[1]
    weights = []
    for mine in range(Y):
        weight = jnp.ones((1, width), F32)
        for other in range(Y):
            if other != mine:
                weight = weight * jnp.where(spots[other] > spots[mine], decays[other], 1.0)
        weights.append(weight)
    whole = decays[0] * decays[1] * decays[2] * decays[3]
    at = lax.broadcasted_iota(jnp.int32, (16, width), 0)
    high = whole.astype(BF16).astype(F32)
    tail = jnp.where(at == 0, high, jnp.where(at == 1, whole - high, 0.0)).astype(BF16)
    lanes_each = out.shape[2]
    for owner in range(out.shape[0]):
        lanes = slice(owner * lanes_each, (owner + 1) * lanes_each)
        total = weights[0][:, lanes] * states[0][0:N, lanes].astype(F32)
        for index in range(1, Y):
            total = total + weights[index][:, lanes] * states[index][0:N, lanes].astype(F32)
        out[owner, 0:N] = total.astype(BF16)
        out[owner, N : N + 16] = tail[:, lanes]


def chain_kernel(ids, totals, out):
    carry = jnp.zeros((N, totals.shape[2]), F32)
    for turn in range(totals.shape[0]):
        out[turn, 0:N] = carry.astype(BF16)
        tail = totals[turn, N : N + 16].astype(F32)
        carry = (tail[0:1] + tail[1:2]) * carry + totals[turn, 0:N].astype(F32)
    final = carry.astype(BF16)
    for turn in range(totals.shape[0]):
        out[turn, N : 2 * N] = final


def prefix_kernel(ids, back, *refs):
    states, outs = refs[0:Y], refs[Y : 2 * Y]
    spots = [lax.rem(ids[2] + index, Y) for index in range(Y)]
    decays = [decay_row(state) for state in states]
    lanes_each = back.shape[2]

    def between(low, high):
        weight = jnp.ones(decays[0].shape, F32)
        for other in range(Y):
            inside = spots[other] < high
            if low is not None:
                inside = jnp.logical_and(inside, spots[other] > low)
            weight = weight * jnp.where(inside, decays[other], 1.0)
        return weight

    for target in range(Y):
        base = between(None, spots[target])
        weights = [
            jnp.where(spots[mine] < spots[target], between(spots[mine], spots[target]), 0.0)
            for mine in range(Y)
        ]
        for owner in range(back.shape[0]):
            lanes = slice(owner * lanes_each, (owner + 1) * lanes_each)
            total = base[:, lanes] * back[owner, 0:N].astype(F32)
            for mine in range(Y):
                if mine != target:
                    total = total + weights[mine][:, lanes] * states[mine][0:N, lanes].astype(F32)
            outs[target][:, lanes] = total.astype(BF16)


def decode_kernel(ids, masks, recent, fresh, taps, steps, log_row, skip, cache, out):
    count, rows_dev, channels = fresh.shape
    heads = steps.shape[1]
    width_dev = heads * P_SIZE
    group_dev = (channels - width_dev) // (2 * N)
    chosen = masks[0, :, 0:1] > 0.5
    second = masks[1, :, 0:1] > 0.5
    chosen_rows, second_rows = chosen[0:rows_dev], second[0:rows_dev]
    rim_rows = CONV - 1
    piece = 1024

    def mixes(start):
        lanes = slice(start, start + piece)
        line = []
        for position in range(rim_rows):
            first = recent[position : position + 1, lanes]
            other = recent[rim_rows + position : rim_rows + position + 1, lanes]
            home = recent[2 * rim_rows + position : 2 * rim_rows + position + 1, lanes]
            line.append(jnp.where(chosen_rows, home, jnp.where(second_rows, other, first)))
        line += [fresh[index, :, lanes].astype(F32) for index in range(count)]
        results = []
        for index in range(count):
            mixture = taps[0:1, lanes] * line[index]
            for position in range(1, CONV):
                mixture = mixture + taps[position : position + 1, lanes] * line[index + position]
            results.append(silu(mixture).astype(BF16).astype(F32))
        return results

    ports = mixes(width_dev)
    half = group_dev * N
    size = softplus(steps[...])
    log_decay = size * -jnp.exp(log_row[...])
    sizes = [size[index * rows_dev : (index + 1) * rows_dev] for index in range(count)]
    logs = [log_decay[index * rows_dev : (index + 1) * rows_dev] for index in range(count)]
    lane = lax.broadcasted_iota(jnp.int32, (rows_dev, heads), 1)
    per_group = heads // group_dev
    stack, spots = [], {}
    total = None
    starts = []
    for index in range(count):
        total = logs[index] if total is None else total + logs[index]
        starts.append(jnp.exp(total))
    start_all = jnp.concatenate(starts, axis=0)
    kept = jnp.where(chosen, 0.0, start_all)
    given = jnp.where(chosen, start_all, 0.0)
    for index in range(count):
        gap = None
        for earlier in range(index, -1, -1):
            product = ports[index][:, half : 2 * half] * ports[earlier][:, 0:half]
            meets = jnp.zeros((rows_dev, heads), F32)
            for group in range(group_dev):
                met = jnp.sum(product[:, group * N : (group + 1) * N], axis=1, keepdims=True)
                meets = jnp.where(lax.div(lane, per_group) == group, met, meets)
            weight = meets * sizes[earlier]
            if earlier == index:
                weight = weight + skip[...]
            else:
                gap = logs[earlier + 1] if gap is None else gap + logs[earlier + 1]
                weight = weight * jnp.exp(gap)
            spots[index, earlier] = count * rows_dev + len(stack) * rows_dev
            stack.append(weight)
    coefficients = paired(jnp.concatenate([kept] + stack, axis=0))
    shared = paired(given)
    reads = jnp.concatenate([port[:, half : 2 * half] for port in ports], axis=0).astype(BF16)
    quarters = width_dev // piece
    per = quarters // group_dev
    for quarter in range(quarters):
        lanes = slice(quarter * piece, (quarter + 1) * piece)
        group = quarter // per
        read = reads[:, group * N : (group + 1) * N]
        wide = dot(coefficients, head_spread(quarter, heads, piece))
        values = mixes(quarter * piece)
        met = jnp.where(
            second, dot_nt(read, cache[1, lanes, :]), dot_nt(read, cache[0, lanes, :])
        )
        results = []
        for index in range(count):
            at = index * rows_dev
            line = wide[at : at + rows_dev] * met[at : at + rows_dev]
            for earlier in range(index + 1):
                spot = spots[index, earlier]
                line = line + wide[spot : spot + rows_dev] * values[earlier]
            results.append(line)
        out[quarter, :, 0:piece] = jnp.concatenate(results, axis=0).astype(BF16)
        out[quarter, :, piece : piece + N] = read
        out[quarter, :, piece + N : piece + N + 2 * heads] = shared


def project_kernel(ids, back, *refs):
    pieces, blocks = refs[0:X], refs[X : X + Y]
    keep, send, final, joined = refs[X + Y : X + Y + 4]
    width = joined.shape[1]
    each = back.shape[2]
    for owner in range(back.shape[0]):
        final[:, owner * each : (owner + 1) * each] = back[owner, N : 2 * N]
    pairs = pieces[0].shape[1] - width - N
    spread = head_spread(ids[2], pairs // 2, width)
    for index in range(X):
        spot = lax.rem(ids[0] + index, X)
        same = lax.rem(spot, 2) == ids[3]
        row = lax.div(spot, 2)
        reads = pieces[index][:, width : width + N]
        given = pieces[index][:, width + N :]
        for start in range(0, width, 256):
            lanes = slice(start, start + 256)
            extra = dot(given, spread[:, lanes]) * dot(reads, final[:, lanes])
            joined[:, lanes] = (pieces[index][:, lanes].astype(F32) + extra).astype(BF16)
        for block in range(Y):
            part = dot(joined[...], blocks[block][...])

            @pl.when(same)
            def _():
                keep[block, row] = part

            @pl.when(jnp.logical_not(same))
            def _():
                send[block, row] = part.astype(BF16)


def shards(
    raw_values,
    state_ports,
    step_raw,
    decay_log,
    skip_gain,
    conv_values,
    conv_ports,
    prompt_slot,
    row_slot,
    cache_states,
    cache_values,
    cache_ports,
    new_values,
    new_ports,
    new_steps,
    out_weight,
):
    length, width_dev = raw_values.shape
    heads = decay_log.shape[0]
    ports_dev = 2 * state_ports.shape[2]
    rim_rows = CONV - 1
    width = width_dev // Y
    count, rows_dev = new_steps.shape[0:2]
    me = lax.axis_index("ctx").astype(jnp.int32)
    part = lax.axis_index("head").astype(jnp.int32)
    my_x, my_z, my_y = me // (Z * Y), me // Y % Z, me % Y
    my_core, my_high = part % 2, part // 2
    ids = jnp.stack([my_x, my_z, my_y, my_core])
    quarters = [(my_y + index) % Y for index in range(Y)]
    quarter_ids = [quarter.reshape(1) for quarter in quarters]

    ports_flat = state_ports.reshape(length, ports_dev)
    tails = jnp.concatenate([raw_values[length - rim_rows :], ports_flat[length - rim_rows :]], axis=1)
    devices = X * Z * Y
    rim = lax.ppermute(tails, "ctx", [(i, i + 1) for i in range(devices - 1)])
    rim = jnp.pad(rim.astype(F32), ((8 - rim_rows, 0), (0, 0)))

    last = devices - 1
    home = tails
    at_z = lax.ppermute(home, "ctx", [(last, place(X - 1, Z - 2, Y - 1))])
    home = jnp.where(my_z == Z - 1, home, at_z)
    moved = home
    for step in range(1, Y):
        moved_y = lax.ppermute(
            home, "ctx", [(place(X - 1, z, Y - 1), place(X - 1, z, Y - 1 - step)) for z in range(Z)]
        )
        moved = jnp.where(my_y == Y - 1 - step, moved_y, moved)
    home = moved
    for step in range(1, X):
        moved_x = lax.ppermute(
            home,
            "ctx",
            [(place(X - 1, z, y), place(X - 1 - step, z, y)) for z in range(Z) for y in range(Y)],
        )
        moved = jnp.where(my_x == X - 1 - step, moved_x, moved)
    home = moved

    taps = jnp.concatenate([conv_values, conv_ports.reshape(CONV, ports_dev)], axis=1).astype(F32)
    log_row = decay_log.reshape(1, heads)
    skip_row = skip_gain.reshape(1, heads)
    skip_wide = jnp.repeat(skip_gain, P_SIZE).reshape(1, width_dev)

    read, write_t, run, row, factor, grow = call(
        ports_kernel,
        (
            sds((SPAN, ports_dev // 2), BF16),
            sds((ports_dev // 2, SPAN), BF16),
            sds((Y, SPAN, heads // Y), F32),
            sds((heads, SPAN), F32),
            sds((SPAN + 16, 2 * heads), BF16),
            sds((SPAN, 2 * heads), BF16),
        ),
        scratch=[pltpu.VMEM((SPAN + 8, ports_dev), F32)],
        n_in=8,
        us=4.0,
    )(ids, ports_flat, rim, taps, step_raw, step_raw.T, log_row, decay_log.reshape(heads, 1))

    states, mixed = [None] * Y, [None] * Y
    for index in (1, 3, 2, 0):
        states[index], mixed[index] = state_call(
            quarter_ids[index], raw_values, rim, taps, factor, write_t
        )
    ring = [states[0], None, None, None]
    for index in (1, 3, 2):
        ring[Y - index] = shifted(states[index], dy=index)

    chosen = row_slot == prompt_slot[0]
    masks = jnp.stack([chosen, row_slot == 1]).astype(F32)
    masks = jnp.broadcast_to(jnp.tile(masks, (1, count))[:, :, None], (2, count * rows_dev, 128))
    slots = cache_values.shape[0]
    recent = jnp.concatenate(
        [
            jnp.concatenate(
                [
                    cache_values.reshape(slots * rim_rows, width_dev),
                    cache_ports.reshape(slots * rim_rows, ports_dev),
                ],
                axis=1,
            ),
            home,
        ],
        axis=0,
    ).astype(F32)
    fresh = jnp.concatenate([new_values, new_ports.reshape(count, rows_dev, ports_dev)], axis=2)
    packed_width = width + N + 2 * heads
    packed = call(
        decode_kernel,
        sds((Y, count * rows_dev, packed_width), BF16),
        n_in=9,
        us=6.0,
    )(
        ids,
        masks,
        recent,
        fresh,
        taps,
        new_steps.reshape(count * rows_dev, heads),
        log_row,
        skip_row,
        cache_states.reshape(slots, width_dev, N),
    )
    by_y = [lax.dynamic_index_in_dim(packed, quarters[0], 0, False), None, None, None]
    for index in range(1, Y):
        by_y[Y - index] = shifted(
            lax.dynamic_index_in_dim(packed, quarters[index], 0, False), dy=index
        )
    turned = jnp.concatenate(by_y + by_y[0 : Y - 1], axis=0)
    ordered = lax.dynamic_slice_in_dim(
        turned, (Y - my_y) % Y * count * rows_dev, Y * count * rows_dev, 0
    )
    both = jnp.concatenate([ordered, shifted(ordered, dz=1)], axis=0)
    pieces = [both] + [shifted(both, dx=-index) for index in range(1, X)]

    withins = [
        within_call(quarter_ids[index], read, write_t, run, row, mixed[index], skip_wide)
        for index in range(Y)
    ]

    owners = X * Z
    each = width // owners
    groups = [[place(x, z, y) for x in range(X) for z in range(Z)] for y in range(Y)]
    totals = call(row_total_kernel, sds((owners, N + 16, each), BF16), n_in=1 + Y, us=2.0)(ids, *ring)
    totals = lax.all_to_all(totals, "ctx", 0, 0, tiled=True, axis_index_groups=groups)
    back = call(chain_kernel, sds((owners, 2 * N, each), BF16), n_in=2, us=1.0)(ids, totals)
    back = lax.all_to_all(back, "ctx", 0, 0, tiled=True, axis_index_groups=groups)
    prefixes = call(
        prefix_kernel, tuple(sds((N, width), BF16) for _ in range(Y)), n_in=2 + Y, us=2.5
    )(ids, back, *ring)
    incoming = [prefixes[0], None, None, None]
    for index in (1, 3, 2):
        incoming[Y - index] = shifted(prefixes[index], dy=index)

    blocks = [lax.dynamic_slice_in_dim(out_weight, quarters[0] * width, width, 0), None, None, None]
    for index in (1, 3, 2):
        blocks[Y - index] = shifted(
            lax.dynamic_slice_in_dim(out_weight, quarters[index] * width, width, 0), dy=index
        )
    piece_rows = both.shape[0]
    cols = out_weight.shape[1]
    keep, send = call(
        project_kernel,
        (sds((Y, X // 2, piece_rows, cols), F32), sds((Y, X // 2, piece_rows, cols), BF16)),
        scratch=[pltpu.VMEM((N, width), BF16), pltpu.VMEM((piece_rows, width), BF16)],
        n_in=2 + X + Y,
        us=6.0,
    )(ids, back, *pieces, *blocks)
    other = lax.ppermute(send, "head", [(i, i ^ 1) for i in range(4)])
    joined = keep + other.astype(F32)
    sums = joined[0]
    for index in (1, 3, 2):
        sums = sums + shifted(joined[index].astype(BF16), dy=index).astype(F32)
    theirs = lax.dynamic_index_in_dim(sums, 1 - my_high, 0, False).astype(BF16)
    mine = lax.dynamic_index_in_dim(sums, my_high, 0, False)
    mine = mine + lax.ppermute(theirs, "head", [(i, i ^ 2) for i in range(4)]).astype(F32)
    mine = mine.astype(BF16).reshape(Z, Y, count, rows_dev, cols)
    mine = jnp.where(my_z == 0, mine, mine[::-1])
    decoded_out = mine.transpose(2, 0, 1, 3, 4).reshape(count, Z * Y * rows_dev, cols)

    scan_out = call(carried_kernel, sds((SPAN, width_dev), BF16), n_in=3 + 2 * Y, us=6.0)(
        ids, grow, read, *withins, *incoming
    )
    return scan_out, decoded_out


def solution(mesh):
    in_specs = (
        P("ctx", "head"),
        P("ctx", None, "head"),
        P("ctx", "head"),
        P("head"),
        P("head"),
        P(None, "head"),
        P(None, None, "head"),
        P("ctx"),
        P("ctx"),
        P("ctx", "head", None, None),
        P("ctx", None, "head"),
        P("ctx", None, None, "head"),
        P(None, "ctx", "head"),
        P(None, "ctx", None, "head"),
        P(None, "ctx", "head"),
        P("head", "ctx"),
    )
    out_specs = (P("ctx", "head"), P(None, "head", "ctx"))
    return jax.shard_map(shards, mesh=mesh, in_specs=in_specs, out_specs=out_specs, check_vma=False)
```

```python
import functools

import jax
import jax.numpy as jnp
from jax import lax
from jax.experimental import pallas as pl
from jax.experimental.pallas import tpu as pltpu
from jax.sharding import PartitionSpec as P

P_SIZE = 64
N = 256
CONV = 4
SPAN = 256
X, Z, Y = 4, 2, 4
F32 = jnp.float32
BF16 = jnp.bfloat16
VMEM_BYTES = 48 * 2**20


def place(x, z, y):
    return (x % X * Z + z % Z) * Y + y % Y


def shifted(value, dx=0, dz=0, dy=0):
    pairs = [
        (place(x, z, y), place(x + dx, z + dz, y + dy))
        for x in range(X)
        for z in range(Z)
        for y in range(Y)
    ]
    return lax.ppermute(value, "ctx", pairs)


def whole(shape):
    return pl.BlockSpec(shape, lambda i, s: (0,) * len(shape))


def call(kernel, ids, ins, outs, scratch=(), after=(), into=None, turns=1):
    def split(entry):
        return entry if isinstance(entry, tuple) else (entry, None, None)

    def spec(entry):
        value, block, at = split(entry)
        if block is None:
            return whole(value.shape)
        return pl.BlockSpec(block, lambda i, s: at(s, i))

    extra = list(after) + ([] if into is None else [into])
    count = len(ins)

    def body(*refs):
        kernel(*refs[: 1 + count], *refs[1 + count + len(extra) :])

    aliases = {} if into is None else {count + len(extra): 0}
    return pl.pallas_call(
        body,
        grid_spec=pltpu.PrefetchScalarGridSpec(
            num_scalar_prefetch=1,
            grid=(turns,),
            in_specs=[spec(entry) for entry in ins]
            + [pl.BlockSpec(memory_space=pl.ANY)] * len(extra),
            out_specs=[spec(entry) for entry in outs],
            scratch_shapes=list(scratch),
        ),
        out_shape=[split(entry)[0] for entry in outs],
        input_output_aliases=aliases,
        compiler_params=pltpu.CompilerParams(vmem_limit_bytes=VMEM_BYTES),
        cost_estimate=pl.CostEstimate(
            flops=10**6, bytes_accessed=10**4, transcendentals=0
        ),
    )(ids, *[split(entry)[0] for entry in ins], *extra)


def sds(shape, dtype):
    return jax.ShapeDtypeStruct(shape, dtype)


def silu(value):
    return value * (0.5 + 0.5 * jnp.tanh(0.5 * value))


def softplus(value):
    return jnp.maximum(value, 0.0) + jnp.log1p(jnp.exp(-jnp.abs(value)))


def halves(value):
    high = value.astype(BF16)
    return high, (value - high.astype(F32)).astype(BF16)


def paired(value):
    high, low = halves(value)
    return jnp.concatenate([high.astype(F32), low.astype(F32)], axis=1).astype(BF16)


def head_spread(quarter, heads, width):
    row = lax.broadcasted_iota(jnp.int32, (2 * heads, width), 0)
    col = lax.broadcasted_iota(jnp.int32, (2 * heads, width), 1)
    first = quarter * (width // P_SIZE)
    match = lax.rem(row, heads) == first + lax.div(col, P_SIZE)
    return jnp.where(match, 1.0, 0.0).astype(BF16)


def dot(a, b):
    return jnp.dot(a, b, preferred_element_type=F32)


def dot_nt(a, b):
    return lax.dot_general(a, b, (((1,), (1,)), ((), ())), preferred_element_type=F32)


def wrapped(ids, index):
    return lax.rem(ids[2] + index, Y)


def tails_kernel(ids, raw, ports, out):
    rim_rows, channels = out.shape
    width_dev = raw.shape[1]
    first = raw.shape[0] - rim_rows
    half = ports.shape[2]
    out[:, 0:width_dev] = raw[...].astype(F32)[first:].astype(BF16)
    both = ports[...].astype(F32)
    for part in range(2):
        at = width_dev + part * half
        out[:, at : at + half] = both[first:, part, :].astype(BF16)


def span_kernel(
    ids, raw, ports, rim, value_taps, port_taps, steps_t, log_row, skip_row,
    read_out, write_t_out, run_out, row_out, grow_out, mixed_out, *refs,
):
    payloads = refs[0:Y]
    done, scr, wide, scaled = refs[Y : Y + 4]
    done[...] = jnp.zeros(done.shape, F32)
    width_dev = raw.shape[1]
    half = ports.shape[1] // 2
    heads = log_row.shape[1]
    width = width_dev // Y
    tap = port_taps[...].astype(F32)
    scr[5:8] = rim[:, width_dev:].astype(F32)
    scr[8 : 8 + SPAN] = ports[...].astype(F32)
    for part in range(2):
        lanes = slice(part * half, (part + 1) * half)
        line = tap[:, part, :]
        mixture = line[0:1] * scr[5 : 5 + SPAN, lanes]
        for position in range(1, CONV):
            mixture = mixture + line[position : position + 1] * scr[
                5 + position : 5 + position + SPAN, lanes
            ]
        mixed = silu(mixture)
        if part == 0:
            write_t_out[...] = mixed.astype(BF16).astype(F32).T.astype(BF16)
        else:
            read_out[...] = mixed.astype(BF16)
    rows = lax.broadcasted_iota(jnp.int32, (SPAN, SPAN), 0)
    cols = lax.broadcasted_iota(jnp.int32, (SPAN, SPAN), 1)
    lower = jnp.where(rows >= cols, 1.0, 0.0)
    size_t = softplus(steps_t[...])
    size = size_t.T
    run = jnp.dot(
        lower, size * -jnp.exp(log_row[...]), precision=lax.Precision.HIGHEST,
        preferred_element_type=F32,
    )
    quarter = heads // Y
    for index in range(Y):
        run_out[index] = run[:, index * quarter : (index + 1) * quarter]
    row_out[...] = run.T - jnp.log(size_t)
    ending = run[SPAN - 1 : SPAN]
    factor = jnp.concatenate(
        [
            paired(size * jnp.exp(ending - run)),
            paired(jnp.broadcast_to(jnp.exp(ending), (16, heads))),
        ],
        axis=0,
    )
    grow_out[0:SPAN] = paired(jnp.exp(run))
    grow_out[SPAN : SPAN + 16] = paired(jnp.broadcast_to(skip_row[...], (16, heads)))
    per = Y * N // half
    step = 32
    for index in (1, 3, 2, 0):
        spot = wrapped(ids, index)
        lanes = pl.ds(pl.multiple_of(spot * width, width), width)
        group = lax.div(spot, per)
        write_t = write_t_out[pl.ds(pl.multiple_of(group * N, N), N), :]
        tap = value_taps[:, lanes].astype(F32)
        scr[5:8] = rim[:, lanes].astype(F32)
        scr[8 : 8 + SPAN] = raw[:, lanes].astype(F32)
        wide[...] = dot(factor, head_spread(spot, heads, width))
        for start in range(0, SPAN, step):
            mixture = tap[0:1] * scr[start + 5 : start + 5 + step]
            for position in range(1, CONV):
                at = start + 5 + position
                mixture = mixture + tap[position : position + 1] * scr[at : at + step]
            mixed = silu(mixture).astype(BF16)
            mixed_out[index, start : start + step] = mixed
            scaled[start : start + step] = (
                mixed.astype(F32) * wide[start : start + step]
            ).astype(BF16)
        for start in range(0, width, 256):
            payloads[index][0:N, start : start + 256] = dot(
                write_t, scaled[:, start : start + 256]
            ).astype(BF16)
        decay = wide[SPAN : SPAN + 16]
        high = decay.astype(BF16).astype(F32)
        at = lax.broadcasted_iota(jnp.int32, decay.shape, 0)
        tail = jnp.where(at == 0, high, jnp.where(at == 1, decay - high, 0.0))
        payloads[index][N : N + 16] = tail.astype(BF16)


def scan_kernel(indices, ids, reads, writes_t, runs, row_lines, grow, mixes, *refs):
    states = refs[0 : len(indices)]
    out, scores, wide = refs[len(indices) :]
    for turn, index in enumerate(indices):

        @pl.when(pl.program_id(0) == turn)
        def _():
            scan_quarter(
                index, ids, reads, writes_t, runs, row_lines, mixes, grow, states[turn], out,
                scores, wide,
            )


def scan_quarter(index, ids, reads, writes_t, runs, row_lines, mixes, grow, state, out, scores, wide):
    mixed = mixes.at[index]
    width = mixed.shape[1]
    spot = wrapped(ids, index)
    group = pl.ds(pl.multiple_of(lax.div(spot * reads.shape[1], Y * N) * N, N), N)
    read = reads[:, group]
    heads = width // P_SIZE
    run = runs[pl.ds(spot, 1)]
    row = row_lines[pl.ds(pl.multiple_of(spot * heads, heads), heads), :]
    scores[...] = dot(read, writes_t[group, :])
    wide[...] = dot(grow[...], head_spread(spot, grow.shape[1] // 2, width))
    for start in range(0, width, 256):
        lanes = slice(start, start + 256)
        wide[0:SPAN, lanes] = wide[0:SPAN, lanes] * dot(read, state[:, lanes])
    half = SPAN // 2
    rows = lax.broadcasted_iota(jnp.int32, (half, half), 0)
    cols = lax.broadcasted_iota(jnp.int32, (half, half), 1)
    causal = rows >= cols
    left = lax.broadcasted_iota(jnp.int32, (half, 2 * P_SIZE), 1) < P_SIZE
    for pair in range(width // (2 * P_SIZE)):
        lanes = slice(pair * 2 * P_SIZE, (pair + 1) * 2 * P_SIZE)
        upper, lower = mixed[0:half, lanes], mixed[half:SPAN, lanes]
        tops, bottoms = [], []
        for member in range(2):
            head = 2 * pair + member
            col = run[0, :, head : head + 1]
            line = row[head : head + 1, :]
            w00 = jnp.where(
                causal, scores[0:half, 0:half] * jnp.exp(col[0:half] - line[:, 0:half]), 0.0
            ).astype(BF16)
            w10 = (scores[half:SPAN, 0:half] * jnp.exp(col[half:SPAN] - line[:, 0:half])).astype(BF16)
            w11 = jnp.where(
                causal,
                scores[half:SPAN, half:SPAN] * jnp.exp(col[half:SPAN] - line[:, half:SPAN]),
                0.0,
            ).astype(BF16)
            tops.append(dot(w00, upper))
            bottoms.append(dot(w10, upper) + dot(w11, lower))
        gain = wide[SPAN : SPAN + 1, lanes]
        out[0:half, lanes] = (
            jnp.where(left, tops[0], tops[1]) + wide[0:half, lanes] + gain * upper.astype(F32)
        ).astype(BF16)
        out[half:SPAN, lanes] = (
            jnp.where(left, bottoms[0], bottoms[1]) + wide[half:SPAN, lanes]
            + gain * lower.astype(F32)
        ).astype(BF16)


def decay_row(payload):
    tail = payload[N : N + 16].astype(F32)
    return tail[0:1] + tail[1:2]


def row_total_kernel(ids, *refs):
    states, out, done = refs[0:Y], refs[Y], refs[Y + 1]
    done[...] = jnp.zeros(done.shape, F32)
    spots = [lax.rem(ids[2] + index, Y) for index in range(Y)]
    decays = [decay_row(state) for state in states]
    width = states[0].shape[1]
    weights = []
    for mine in range(Y):
        weight = jnp.ones((1, width), F32)
        for other in range(Y):
            if other != mine:
                weight = weight * jnp.where(spots[other] > spots[mine], decays[other], 1.0)
        weights.append(weight)
    whole = decays[0] * decays[1] * decays[2] * decays[3]
    at = lax.broadcasted_iota(jnp.int32, (16, width), 0)
    high = whole.astype(BF16).astype(F32)
    tail = jnp.where(at == 0, high, jnp.where(at == 1, whole - high, 0.0)).astype(BF16)
    lanes_each = out.shape[2]
    for owner in range(out.shape[0]):
        lanes = slice(owner * lanes_each, (owner + 1) * lanes_each)
        total = weights[0][:, lanes] * states[0][0:N, lanes].astype(F32)
        for index in range(1, Y):
            total = total + weights[index][:, lanes] * states[index][0:N, lanes].astype(F32)
        out[owner, 0:N] = total.astype(BF16)
        out[owner, N : N + 16] = tail[:, lanes]


def chain_kernel(ids, totals, out):
    carry = jnp.zeros((N, totals.shape[2]), F32)
    for turn in range(totals.shape[0]):
        out[turn, 0:N] = carry.astype(BF16)
        tail = totals[turn, N : N + 16].astype(F32)
        carry = (tail[0:1] + tail[1:2]) * carry + totals[turn, 0:N].astype(F32)
    final = carry.astype(BF16)
    for turn in range(totals.shape[0]):
        out[turn, N : 2 * N] = final


def prefix_kernel(ids, back, *refs):
    states, outs = refs[0:Y], refs[Y : 2 * Y]
    spots = [lax.rem(ids[2] + index, Y) for index in range(Y)]
    decays = [decay_row(state) for state in states]
    lanes_each = back.shape[2]

    def between(low, high):
        weight = jnp.ones(decays[0].shape, F32)
        for other in range(Y):
            inside = spots[other] < high
            if low is not None:
                inside = jnp.logical_and(inside, spots[other] > low)
            weight = weight * jnp.where(inside, decays[other], 1.0)
        return weight

    for target in range(Y):
        base = between(None, spots[target])
        weights = [
            jnp.where(spots[mine] < spots[target], between(spots[mine], spots[target]), 0.0)
            for mine in range(Y)
        ]
        for owner in range(back.shape[0]):
            lanes = slice(owner * lanes_each, (owner + 1) * lanes_each)
            total = base[:, lanes] * back[owner, 0:N].astype(F32)
            for mine in range(Y):
                if mine != target:
                    total = total + weights[mine][:, lanes] * states[mine][0:N, lanes].astype(F32)
            outs[target][:, lanes] = total.astype(BF16)


def decode_kernel(
    ids, home, home_1, home_2, home_3, old_values, old_ports, new_values, new_ports,
    value_taps, port_taps, steps, log_row, skip, cache, out,
):
    count, rows_dev, width_dev = new_values.shape
    heads = steps.shape[1]
    group_dev = new_ports.shape[3] // N
    rim_rows = CONV - 1
    piece = out.shape[2] - N - 2 * heads
    at = lax.broadcasted_iota(jnp.int32, (count * rows_dev, 1), 0)
    slot = jnp.zeros(at.shape, jnp.int32)
    for spot in range(rows_dev):
        slot = jnp.where(lax.rem(at, rows_dev) == spot, ids[6 + spot], slot)
    chosen = slot == ids[5]
    second = slot == 1
    chosen_rows, second_rows = chosen[0:rows_dev], second[0:rows_dev]
    tails = home[...].astype(F32)
    for back, other in ((1, home_1), (2, home_2), (3, home_3)):
        tails = jnp.where(ids[0] == X - 1 - back, other[...].astype(F32), tails)

    def mix(tap, lines):
        results = []
        for index in range(count):
            mixture = tap[0:1] * lines[index]
            for position in range(1, CONV):
                mixture = mixture + tap[position : position + 1] * lines[index + position]
            results.append(silu(mixture).astype(BF16).astype(F32))
        return results

    def pick(first, other, prompt):
        return jnp.where(chosen_rows, prompt, jnp.where(second_rows, other, first))

    def value_mixes(lanes):
        lines = []
        for position in range(rim_rows):
            old = old_values[position, :, lanes].astype(F32)
            lines.append(pick(old[0:1], old[1:2], tails[position : position + 1, lanes]))
        lines += [new_values[index, :, lanes].astype(F32) for index in range(count)]
        return mix(value_taps[:, lanes].astype(F32), lines)

    def port_mixes(part):
        lines = []
        width = group_dev * N
        lanes = slice(width_dev + part * width, width_dev + (part + 1) * width)
        for position in range(rim_rows):
            old = [old_ports[member, position].astype(F32)[part : part + 1] for member in range(2)]
            lines.append(pick(old[0], old[1], tails[position : position + 1, lanes]))
        lines += [new_ports[index].astype(F32)[:, part, :] for index in range(count)]
        return mix(port_taps[...].astype(F32)[:, part, :], lines)

    writes, read_rows = port_mixes(0), port_mixes(1)
    size = softplus(steps[...])
    log_decay = size * -jnp.exp(log_row[...])
    sizes = [size[index * rows_dev : (index + 1) * rows_dev] for index in range(count)]
    logs = [log_decay[index * rows_dev : (index + 1) * rows_dev] for index in range(count)]
    lane = lax.broadcasted_iota(jnp.int32, (rows_dev, heads), 1)
    per_group = heads // group_dev
    stack, spots = [], {}
    total = None
    starts = []
    for index in range(count):
        total = logs[index] if total is None else total + logs[index]
        starts.append(jnp.exp(total))
    start_all = jnp.concatenate(starts, axis=0)
    kept = jnp.where(chosen, 0.0, start_all)
    given = jnp.where(chosen, start_all, 0.0)
    for index in range(count):
        gap = None
        for earlier in range(index, -1, -1):
            product = read_rows[index] * writes[earlier]
            meets = jnp.zeros((rows_dev, heads), F32)
            for group in range(group_dev):
                met = jnp.sum(product[:, group * N : (group + 1) * N], axis=1, keepdims=True)
                meets = jnp.where(lax.div(lane, per_group) == group, met, meets)
            weight = meets * sizes[earlier]
            if earlier == index:
                weight = weight + skip[...]
            else:
                gap = logs[earlier + 1] if gap is None else gap + logs[earlier + 1]
                weight = weight * jnp.exp(gap)
            spots[index, earlier] = count * rows_dev + len(stack) * rows_dev
            stack.append(weight)
    coefficients = paired(jnp.concatenate([kept] + stack, axis=0))
    shared = paired(given)
    reads = jnp.concatenate(read_rows, axis=0).astype(BF16)
    quarters = width_dev // piece
    per = quarters // group_dev
    for quarter in range(quarters):
        lanes = slice(quarter * piece, (quarter + 1) * piece)
        group = quarter // per
        read = reads[:, group * N : (group + 1) * N]
        wide = dot(coefficients, head_spread(quarter, heads, piece))
        values = value_mixes(lanes)
        met = jnp.where(
            second, dot_nt(read, cache[1, lanes, :]), dot_nt(read, cache[0, lanes, :])
        )
        results = []
        for index in range(count):
            at = index * rows_dev
            line = wide[at : at + rows_dev] * met[at : at + rows_dev]
            for earlier in range(index + 1):
                spot = spots[index, earlier]
                line = line + wide[spot : spot + rows_dev] * values[earlier]
            results.append(line)
        out[quarter, :, 0:piece] = jnp.concatenate(results, axis=0).astype(BF16)
        out[quarter, :, piece : piece + N] = read
        out[quarter, :, piece + N : piece + N + 2 * heads] = shared


def copy_kernel(ids, source, out):
    out[...] = source[...]


def order_kernel(ids, *refs):
    out, done = refs[Y : Y + 2]
    done[...] = jnp.zeros(done.shape, F32)
    for index in range(Y):
        out[wrapped(ids, index)] = refs[index][...]


def project_kernel(ids, back, *refs):
    pieces, blocks = refs[0 : Z * X], refs[Z * X : Z * X + Y]
    keep, send, final, joined = refs[Z * X + Y : Z * X + Y + 4]
    width = joined.shape[1]
    each = back.shape[2]
    rows = pieces[0].shape[0]
    for owner in range(back.shape[0]):
        final[:, owner * each : (owner + 1) * each] = back[owner, N : 2 * N]
    pairs = pieces[0].shape[1] - width - N
    spread = head_spread(ids[2], pairs // 2, width)
    for index in range(X):
        for member in range(Z):
            piece = pieces[member * X + index]
            at = (index * Z + member) * rows
            for start in range(0, width, 256):
                lanes = slice(start, start + 256)
                extra = dot(piece[:, width + N :], spread[:, lanes]) * dot(
                    piece[:, width : width + N], final[:, lanes]
                )
                joined[at : at + rows, lanes] = (piece[:, lanes].astype(F32) + extra).astype(BF16)
    for block in range(Y):
        part = dot(joined[...], blocks[block][...]).astype(BF16)
        for index in range(X):
            spot = lax.rem(ids[0] + index, X)
            same = lax.rem(spot, 2) == ids[3]
            row = lax.div(spot, 2)
            lines = part[index * Z * rows : (index + 1) * Z * rows]

            @pl.when(same)
            def _():
                keep[block, row] = lines

            @pl.when(jnp.logical_not(same))
            def _():
                send[block, row] = lines


def pair_sum_kernel(ids, keep, other, own, *outs):
    own[...] = keep[0].astype(F32) + other[0].astype(F32)
    for index in range(1, Y):
        outs[index - 1][...] = (keep[index].astype(F32) + other[index].astype(F32)).astype(BF16)


def ring_sum_kernel(ids, own, first, second, third, mine, theirs):
    high = ids[4]

    def total(at):
        return (
            own[at] + first[at].astype(F32) + second[at].astype(F32) + third[at].astype(F32)
        )

    mine[...] = total(high)
    theirs[...] = total(1 - high).astype(BF16)


def finish_kernel(ids, mine, other, out):
    total = mine[...] + other[...].astype(F32)
    count = out.shape[0]
    rows = out.shape[1] // (Z * Y)
    for member in range(Z):
        spot = lax.rem(ids[1] + member, Z)
        for index in range(count):
            lines = []
            for turn in range(Y):
                at = ((member * Y + turn) * count + index) * rows
                lines.append(total[at : at + rows])
            out[index, pl.ds(pl.multiple_of(spot * Y * rows, Y * rows), Y * rows), :] = (
                jnp.concatenate(lines, axis=0).astype(BF16)
            )


def shards(
    raw_values,
    state_ports,
    step_raw,
    decay_log,
    skip_gain,
    conv_values,
    conv_ports,
    prompt_slot,
    row_slot,
    cache_states,
    cache_values,
    cache_ports,
    new_values,
    new_ports,
    new_steps,
    out_weight,
):
    length, width_dev = raw_values.shape
    heads = decay_log.shape[0]
    ports_dev = 2 * state_ports.shape[2]
    rim_rows = CONV - 1
    width = width_dev // Y
    count, rows_dev = new_steps.shape[0:2]
    per = Y * N // state_ports.shape[2]
    me = lax.axis_index("ctx").astype(jnp.int32)
    part = lax.axis_index("head").astype(jnp.int32)
    my_x, my_z, my_y = me // (Z * Y), me // Y % Z, me % Y
    my_core, my_high = part % 2, part // 2
    ids = jnp.concatenate(
        [jnp.stack([my_x, my_z, my_y, my_core, my_high]), prompt_slot, row_slot]
    )
    devices = X * Z * Y
    log_row = decay_log.reshape(1, heads)
    skip_row = skip_gain.reshape(1, heads)

    def quarter_block(block, index, dim):
        def at(s, i):
            spot = [0] * len(block)
            spot[dim] = wrapped(s, index)
            return tuple(spot)

        return block, at

    edge = 16
    last_edge = length // edge - 1
    tails = call(
        tails_kernel,
        ids,
        [
            (raw_values, (edge, width_dev), lambda s, i: (last_edge, 0)),
            (state_ports, (edge,) + state_ports.shape[1:], lambda s, i: (last_edge, 0, 0)),
        ],
        [sds((rim_rows, width_dev + ports_dev), BF16)],
    )[0]
    rim = lax.ppermute(tails, "ctx", [(i, i + 1) for i in range(devices - 1)])
    last = devices - 1
    moved = tails
    for step in range(1, Y):
        at_y = lax.ppermute(tails, "ctx", [(last, last - step)])
        moved = jnp.where(my_y == Y - 1 - step, at_y, moved)
    home_y = moved
    at_z = lax.ppermute(
        home_y, "ctx", [(place(X - 1, Z - 1, y), place(X - 1, 0, y)) for y in range(Y)]
    )
    moved = jnp.where(my_z == Z - 1, home_y, at_z)
    homes = [moved]
    for step in range(1, X):
        homes.append(
            lax.ppermute(
                moved,
                "ctx",
                [(place(X - 1, z, y), place(X - 1 - step, z, y)) for z in range(Z) for y in range(Y)],
            )
        )

    span = call(
        span_kernel,
        ids,
        [
            raw_values,
            state_ports.reshape(length, ports_dev),
            rim,
            conv_values,
            conv_ports,
            step_raw.T,
            log_row,
            skip_row,
        ],
        [
            sds((SPAN, ports_dev // 2), BF16),
            sds((ports_dev // 2, SPAN), BF16),
            sds((Y, SPAN, heads // Y), F32),
            sds((heads, SPAN), F32),
            sds((SPAN + 16, 2 * heads), BF16),
            sds((Y, SPAN, width), BF16),
        ]
        + [sds((N + 16, width), BF16)] * Y
        + [sds((8, 128), F32)],
        scratch=[
            pltpu.VMEM((SPAN + 8, width), F32),
            pltpu.VMEM((SPAN + 16, width), F32),
            pltpu.VMEM((SPAN, width), BF16),
        ],
    )
    shared, states, spanned = span[0:6], span[6 : 6 + Y], span[6 + Y]
    ring = [states[0], None, None, None]
    for index in (1, 3, 2):
        ring[Y - index] = shifted(states[index], dy=index)

    packed_width = width + N + 2 * heads
    slots = cache_states.shape[0]
    packed = call(
        decode_kernel,
        ids,
        [
            *homes,
            cache_values.transpose(1, 0, 2),
            cache_ports,
            new_values,
            new_ports,
            conv_values,
            conv_ports,
            new_steps.reshape(count * rows_dev, heads),
            log_row,
            skip_row,
            cache_states.reshape(slots, width_dev, N),
        ],
        [sds((Y, count * rows_dev, packed_width), BF16)],
        after=[spanned],
    )[0]
    quarters = [(my_y + index) % Y for index in range(Y)]
    by_y = [lax.dynamic_index_in_dim(packed, quarters[0], 0, False), None, None, None]
    for index in range(1, Y):
        by_y[Y - index] = shifted(
            lax.dynamic_index_in_dim(packed, quarters[index], 0, False), dy=index
        )
    ordered, turned = call(
        order_kernel,
        ids,
        by_y,
        [sds((Y, count * rows_dev, packed_width), BF16), sds((8, 128), F32)],
    )
    piece_rows = Z * Y * count * rows_dev
    pieces = []
    for held in (ordered, shifted(ordered, dz=1)):
        held = held.reshape(Y * count * rows_dev, packed_width)
        pieces += [held] + [shifted(held, dx=-index) for index in range(1, X)]

    owners = X * Z
    each = width // owners
    groups = [[place(x, z, y) for x in range(X) for z in range(Z)] for y in range(Y)]
    totals, summed = call(
        row_total_kernel,
        ids,
        ring,
        [sds((owners, N + 16, each), BF16), sds((8, 128), F32)],
        after=[turned],
    )
    totals = lax.all_to_all(totals, "ctx", 0, 0, tiled=True, axis_index_groups=groups)
    back = call(chain_kernel, ids, [totals], [sds((owners, 2 * N, each), BF16)])[0]
    back = lax.all_to_all(back, "ctx", 0, 0, tiled=True, axis_index_groups=groups)
    prefixes = call(
        prefix_kernel,
        ids,
        [back, *ring],
        [sds((N, width), BF16) for _ in range(Y)],
    )
    incoming = [prefixes[0], None, None, None]
    for index in (1, 3, 2):
        incoming[Y - index] = shifted(prefixes[index], dy=index)

    def weight_block(index, after=()):
        return call(
            copy_kernel,
            ids,
            [(out_weight, *quarter_block((width, out_weight.shape[1]), index, 0))],
            [sds((width, out_weight.shape[1]), BF16)],
            after=after,
        )[0]

    blocks = [None] * Y
    for index in (1, 3, 2):
        blocks[Y - index] = shifted(weight_block(index, after=[summed]), dy=index)

    cols = out_weight.shape[1]
    keep, send = call(
        project_kernel,
        ids,
        [
            back,
            *pieces,
            (out_weight, *quarter_block((width, cols), 0, 0)),
            *blocks[1:],
        ],
        [sds((Y, X // 2, piece_rows, cols), BF16)] * 2,
        scratch=[pltpu.VMEM((N, width), BF16), pltpu.VMEM((X * piece_rows, width), BF16)],
        after=[incoming[1][0:16, 0:128], incoming[3][0:16, 0:128]],
    )
    other = lax.ppermute(send, "head", [(i, i ^ 1) for i in range(4)])
    half = (X // 2, piece_rows, cols)
    own, *outward = call(
        pair_sum_kernel,
        ids,
        [keep, other],
        [sds(half, F32)] + [sds(half, BF16)] * (Y - 1),
    )
    inward = [shifted(outward[index - 1], dy=index) for index in (1, 3, 2)]
    mine, theirs = call(
        ring_sum_kernel, ids, [own, *inward], [sds(half[1:], F32), sds(half[1:], BF16)]
    )
    other = lax.ppermute(theirs, "head", [(i, i ^ 2) for i in range(4)])
    decoded_out = call(
        finish_kernel, ids, [mine, other], [sds((count, Z * Y * rows_dev, cols), BF16)]
    )[0]

    def turn_block(indices):
        def at(s, i):
            index = indices[0]
            for turn in range(1, len(indices)):
                index = jnp.where(i == turn, indices[turn], index)
            return 0, wrapped(s, index)

        return at

    scan_out = None
    for indices in ((0, 1, 3), (2,)):
        scan_out = call(
            functools.partial(scan_kernel, indices),
            ids,
            [*shared, *[incoming[index] for index in indices]],
            [(sds((SPAN, width_dev), BF16), (SPAN, width), turn_block(indices))],
            scratch=[pltpu.VMEM((SPAN, SPAN), F32), pltpu.VMEM((SPAN + 16, width), F32)],
            into=scan_out,
            turns=len(indices),
        )[0]
    return scan_out, decoded_out


def solution(mesh):
    in_specs = (
        P("ctx", "head"),
        P("ctx", None, "head"),
        P("ctx", "head"),
        P("head"),
        P("head"),
        P(None, "head"),
        P(None, None, "head"),
        P("ctx"),
        P("ctx"),
        P("ctx", "head", None, None),
        P("ctx", None, "head"),
        P("ctx", None, None, "head"),
        P(None, "ctx", "head"),
        P(None, "ctx", None, "head"),
        P(None, "ctx", "head"),
        P("head", "ctx"),
    )
    out_specs = (P("ctx", "head"), P(None, "head", "ctx"))
    return jax.shard_map(shards, mesh=mesh, in_specs=in_specs, out_specs=out_specs, check_vma=False)
```

```python
import functools

import jax
import jax.numpy as jnp
from jax import lax
from jax.experimental import pallas as pl
from jax.experimental.pallas import tpu as pltpu
from jax.sharding import PartitionSpec as P

P_SIZE = 64
N = 256
CONV = 4
SPAN = 256
X, Z, Y = 4, 2, 4
F32 = jnp.float32
BF16 = jnp.bfloat16
VMEM_BYTES = 24 * 2**20


def place(x, z, y):
    return (x % X * Z + z % Z) * Y + y % Y


def shifted(value, dx=0, dz=0, dy=0):
    pairs = [
        (place(x, z, y), place(x + dx, z + dz, y + dy))
        for x in range(X)
        for z in range(Z)
        for y in range(Y)
    ]
    return lax.ppermute(value, "ctx", pairs)


def whole(shape):
    return pl.BlockSpec(shape, lambda i, s: (0,) * len(shape))


def call(kernel, ids, ins, outs, scratch=(), after=(), into=None, turns=1):
    def split(entry):
        return entry if isinstance(entry, tuple) else (entry, None, None)

    def spec(entry):
        value, block, at = split(entry)
        if block is None:
            return whole(value.shape)
        return pl.BlockSpec(block, lambda i, s: at(s, i))

    extra = list(after) + ([] if into is None else [into])
    count = len(ins)

    def body(*refs):
        kernel(*refs[: 1 + count], *refs[1 + count + len(extra) :])

    aliases = {} if into is None else {count + len(extra): 0}
    return pl.pallas_call(
        body,
        grid_spec=pltpu.PrefetchScalarGridSpec(
            num_scalar_prefetch=1,
            grid=(turns,),
            in_specs=[spec(entry) for entry in ins]
            + [pl.BlockSpec(memory_space=pl.ANY)] * len(extra),
            out_specs=[spec(entry) for entry in outs],
            scratch_shapes=list(scratch),
        ),
        out_shape=[split(entry)[0] for entry in outs],
        input_output_aliases=aliases,
        compiler_params=pltpu.CompilerParams(vmem_limit_bytes=VMEM_BYTES),
        cost_estimate=pl.CostEstimate(
            flops=4 * 10**9, bytes_accessed=10**4, transcendentals=0
        ),
    )(ids, *[split(entry)[0] for entry in ins], *extra)


def sds(shape, dtype):
    return jax.ShapeDtypeStruct(shape, dtype)


def silu(value):
    return value * (0.5 + 0.5 * jnp.tanh(0.5 * value))


def softplus(value):
    return jnp.maximum(value, 0.0) + jnp.log1p(jnp.exp(-jnp.abs(value)))


def halves(value):
    high = value.astype(BF16)
    return high, (value - high.astype(F32)).astype(BF16)


def paired(value):
    high, low = halves(value)
    return jnp.concatenate([high.astype(F32), low.astype(F32)], axis=1).astype(BF16)


def head_spread(quarter, heads, width):
    row = lax.broadcasted_iota(jnp.int32, (2 * heads, width), 0)
    col = lax.broadcasted_iota(jnp.int32, (2 * heads, width), 1)
    first = quarter * (width // P_SIZE)
    match = lax.rem(row, heads) == first + lax.div(col, P_SIZE)
    return jnp.where(match, 1.0, 0.0).astype(BF16)


def dot(a, b):
    return jnp.dot(a, b, preferred_element_type=F32)


def dot_nt(a, b):
    return lax.dot_general(a, b, (((1,), (1,)), ((), ())), preferred_element_type=F32)


def wrapped(ids, index):
    return lax.rem(ids[2] + index, Y)


def tails_kernel(ids, raw, ports, out):
    rim_rows, channels = out.shape
    width_dev = raw.shape[1]
    first = raw.shape[0] - rim_rows
    half = ports.shape[2]
    out[:, 0:width_dev] = raw[...].astype(F32)[first:].astype(BF16)
    both = ports[...].astype(F32)
    for part in range(2):
        at = width_dev + part * half
        out[:, at : at + half] = both[first:, part, :].astype(BF16)


def span_kernel(
    ids, raw, ports, rim, value_taps, port_taps, steps_t, log_row, skip_row,
    read_out, write_t_out, run_out, row_out, grow_out, mixed_out, *refs,
):
    payloads = refs[0:Y]
    done, scr, wide, scaled = refs[Y : Y + 4]
    done[...] = jnp.zeros(done.shape, F32)
    width_dev = raw.shape[1]
    half = ports.shape[1] // 2
    heads = log_row.shape[1]
    width = width_dev // Y
    tap = port_taps[...].astype(F32)
    scr[5:8] = rim[:, width_dev:].astype(F32)
    scr[8 : 8 + SPAN] = ports[...].astype(F32)
    for part in range(2):
        lanes = slice(part * half, (part + 1) * half)
        line = tap[:, part, :]
        mixture = line[0:1] * scr[5 : 5 + SPAN, lanes]
        for position in range(1, CONV):
            mixture = mixture + line[position : position + 1] * scr[
                5 + position : 5 + position + SPAN, lanes
            ]
        mixed = silu(mixture)
        if part == 0:
            write_t_out[...] = mixed.astype(BF16).astype(F32).T.astype(BF16)
        else:
            read_out[...] = mixed.astype(BF16)
    rows = lax.broadcasted_iota(jnp.int32, (SPAN, SPAN), 0)
    cols = lax.broadcasted_iota(jnp.int32, (SPAN, SPAN), 1)
    lower = jnp.where(rows >= cols, 1.0, 0.0)
    size_t = softplus(steps_t[...])
    size = size_t.T
    run = jnp.dot(
        lower, size * -jnp.exp(log_row[...]), precision=lax.Precision.HIGHEST,
        preferred_element_type=F32,
    )
    quarter = heads // Y
    for index in range(Y):
        run_out[index] = run[:, index * quarter : (index + 1) * quarter]
    row_out[...] = run.T - jnp.log(size_t)
    ending = run[SPAN - 1 : SPAN]
    factor = jnp.concatenate(
        [
            paired(size * jnp.exp(ending - run)),
            paired(jnp.broadcast_to(jnp.exp(ending), (16, heads))),
        ],
        axis=0,
    )
    grow_out[0:SPAN] = paired(jnp.exp(run))
    grow_out[SPAN : SPAN + 16] = paired(jnp.broadcast_to(skip_row[...], (16, heads)))
    per = Y * N // half
    step = 32
    for index in (1, 3, 2, 0):
        spot = wrapped(ids, index)
        lanes = pl.ds(pl.multiple_of(spot * width, width), width)
        group = lax.div(spot, per)
        write_t = write_t_out[pl.ds(pl.multiple_of(group * N, N), N), :]
        tap = value_taps[:, lanes].astype(F32)
        scr[5:8] = rim[:, lanes].astype(F32)
        scr[8 : 8 + SPAN] = raw[:, lanes].astype(F32)
        wide[...] = dot(factor, head_spread(spot, heads, width))
        for start in range(0, SPAN, step):
            mixture = tap[0:1] * scr[start + 5 : start + 5 + step]
            for position in range(1, CONV):
                at = start + 5 + position
                mixture = mixture + tap[position : position + 1] * scr[at : at + step]
            mixed = silu(mixture).astype(BF16)
            mixed_out[index, start : start + step] = mixed
            scaled[start : start + step] = (
                mixed.astype(F32) * wide[start : start + step]
            ).astype(BF16)
        for start in range(0, width, 256):
            payloads[index][0:N, start : start + 256] = dot(
                write_t, scaled[:, start : start + 256]
            ).astype(BF16)
        decay = wide[SPAN : SPAN + 16]
        high = decay.astype(BF16).astype(F32)
        at = lax.broadcasted_iota(jnp.int32, decay.shape, 0)
        tail = jnp.where(at == 0, high, jnp.where(at == 1, decay - high, 0.0))
        payloads[index][N : N + 16] = tail.astype(BF16)


def scan_kernel(indices, ids, reads, writes_t, runs, row_lines, grow, mixes, *refs):
    states = refs[0 : len(indices)]
    out, scores, wide = refs[len(indices) :]
    for turn, index in enumerate(indices):

        @pl.when(pl.program_id(0) == turn)
        def _():
            scan_quarter(
                index, ids, reads, writes_t, runs, row_lines, mixes, grow, states[turn], out,
                scores, wide,
            )


def scan_quarter(index, ids, reads, writes_t, runs, row_lines, mixes, grow, state, out, scores, wide):
    mixed = mixes.at[index]
    width = mixed.shape[1]
    spot = wrapped(ids, index)
    group = pl.ds(pl.multiple_of(lax.div(spot * reads.shape[1], Y * N) * N, N), N)
    read = reads[:, group]
    heads = width // P_SIZE
    run = runs[pl.ds(spot, 1)]
    row = row_lines[pl.ds(pl.multiple_of(spot * heads, heads), heads), :]
    scores[...] = dot(read, writes_t[group, :])
    wide[...] = dot(grow[...], head_spread(spot, grow.shape[1] // 2, width))
    for start in range(0, width, 256):
        lanes = slice(start, start + 256)
        wide[0:SPAN, lanes] = wide[0:SPAN, lanes] * dot(read, state[:, lanes])
    half = SPAN // 2
    rows = lax.broadcasted_iota(jnp.int32, (half, half), 0)
    cols = lax.broadcasted_iota(jnp.int32, (half, half), 1)
    causal = rows >= cols
    left = lax.broadcasted_iota(jnp.int32, (half, 2 * P_SIZE), 1) < P_SIZE
    for pair in range(width // (2 * P_SIZE)):
        lanes = slice(pair * 2 * P_SIZE, (pair + 1) * 2 * P_SIZE)
        upper, lower = mixed[0:half, lanes], mixed[half:SPAN, lanes]
        tops, bottoms = [], []
        for member in range(2):
            head = 2 * pair + member
            col = run[0, :, head : head + 1]
            line = row[head : head + 1, :]
            w00 = jnp.where(
                causal, scores[0:half, 0:half] * jnp.exp(col[0:half] - line[:, 0:half]), 0.0
            ).astype(BF16)
            w10 = (scores[half:SPAN, 0:half] * jnp.exp(col[half:SPAN] - line[:, 0:half])).astype(BF16)
            w11 = jnp.where(
                causal,
                scores[half:SPAN, half:SPAN] * jnp.exp(col[half:SPAN] - line[:, half:SPAN]),
                0.0,
            ).astype(BF16)
            tops.append(dot(w00, upper))
            bottoms.append(dot(w10, upper) + dot(w11, lower))
        gain = wide[SPAN : SPAN + 1, lanes]
        out[0:half, lanes] = (
            jnp.where(left, tops[0], tops[1]) + wide[0:half, lanes] + gain * upper.astype(F32)
        ).astype(BF16)
        out[half:SPAN, lanes] = (
            jnp.where(left, bottoms[0], bottoms[1]) + wide[half:SPAN, lanes]
            + gain * lower.astype(F32)
        ).astype(BF16)


def decay_row(payload):
    tail = payload[N : N + 16].astype(F32)
    return tail[0:1] + tail[1:2]


def row_total_kernel(ids, *refs):
    states, out, done = refs[0:Y], refs[Y], refs[Y + 1]
    done[...] = jnp.zeros(done.shape, F32)
    spots = [lax.rem(ids[2] + index, Y) for index in range(Y)]
    decays = [decay_row(state) for state in states]
    width = states[0].shape[1]
    weights = []
    for mine in range(Y):
        weight = jnp.ones((1, width), F32)
        for other in range(Y):
            if other != mine:
                weight = weight * jnp.where(spots[other] > spots[mine], decays[other], 1.0)
        weights.append(weight)
    whole = decays[0] * decays[1] * decays[2] * decays[3]
    at = lax.broadcasted_iota(jnp.int32, (16, width), 0)
    high = whole.astype(BF16).astype(F32)
    tail = jnp.where(at == 0, high, jnp.where(at == 1, whole - high, 0.0)).astype(BF16)
    lanes_each = out.shape[2]
    for owner in range(out.shape[0]):
        lanes = slice(owner * lanes_each, (owner + 1) * lanes_each)
        total = weights[0][:, lanes] * states[0][0:N, lanes].astype(F32)
        for index in range(1, Y):
            total = total + weights[index][:, lanes] * states[index][0:N, lanes].astype(F32)
        out[owner, 0:N] = total.astype(BF16)
        out[owner, N : N + 16] = tail[:, lanes]


def chain_kernel(ids, totals, out):
    carry = jnp.zeros((N, totals.shape[2]), F32)
    for turn in range(totals.shape[0]):
        out[turn, 0:N] = carry.astype(BF16)
        tail = totals[turn, N : N + 16].astype(F32)
        carry = (tail[0:1] + tail[1:2]) * carry + totals[turn, 0:N].astype(F32)
    final = carry.astype(BF16)
    for turn in range(totals.shape[0]):
        out[turn, N : 2 * N] = final


def prefix_kernel(ids, back, *refs):
    states, outs = refs[0:Y], refs[Y : 2 * Y]
    spots = [lax.rem(ids[2] + index, Y) for index in range(Y)]
    decays = [decay_row(state) for state in states]
    lanes_each = back.shape[2]

    def between(low, high):
        weight = jnp.ones(decays[0].shape, F32)
        for other in range(Y):
            inside = spots[other] < high
            if low is not None:
                inside = jnp.logical_and(inside, spots[other] > low)
            weight = weight * jnp.where(inside, decays[other], 1.0)
        return weight

    for target in range(Y):
        base = between(None, spots[target])
        weights = [
            jnp.where(spots[mine] < spots[target], between(spots[mine], spots[target]), 0.0)
            for mine in range(Y)
        ]
        for owner in range(back.shape[0]):
            lanes = slice(owner * lanes_each, (owner + 1) * lanes_each)
            total = base[:, lanes] * back[owner, 0:N].astype(F32)
            for mine in range(Y):
                if mine != target:
                    total = total + weights[mine][:, lanes] * states[mine][0:N, lanes].astype(F32)
            outs[target][:, lanes] = total.astype(BF16)


def decode_kernel(
    ids, home, home_1, home_2, home_3, old_values, old_ports, new_values, new_ports,
    value_taps, port_taps, steps, log_row, skip, cache, out,
):
    count, rows_dev, width_dev = new_values.shape
    heads = steps.shape[1]
    group_dev = new_ports.shape[3] // N
    rim_rows = CONV - 1
    piece = out.shape[2] - N - 2 * heads
    at = lax.broadcasted_iota(jnp.int32, (count * rows_dev, 1), 0)
    slot = jnp.zeros(at.shape, jnp.int32)
    for spot in range(rows_dev):
        slot = jnp.where(lax.rem(at, rows_dev) == spot, ids[6 + spot], slot)
    chosen = slot == ids[5]
    second = slot == 1
    chosen_rows, second_rows = chosen[0:rows_dev], second[0:rows_dev]
    tails = home[...].astype(F32)
    for back, other in ((1, home_1), (2, home_2), (3, home_3)):
        tails = jnp.where(ids[0] == X - 1 - back, other[...].astype(F32), tails)

    def mix(tap, lines):
        results = []
        for index in range(count):
            mixture = tap[0:1] * lines[index]
            for position in range(1, CONV):
                mixture = mixture + tap[position : position + 1] * lines[index + position]
            results.append(silu(mixture).astype(BF16).astype(F32))
        return results

    def pick(first, other, prompt):
        return jnp.where(chosen_rows, prompt, jnp.where(second_rows, other, first))

    def value_mixes(lanes):
        lines = []
        for position in range(rim_rows):
            old = old_values[position, :, lanes].astype(F32)
            lines.append(pick(old[0:1], old[1:2], tails[position : position + 1, lanes]))
        lines += [new_values[index, :, lanes].astype(F32) for index in range(count)]
        return mix(value_taps[:, lanes].astype(F32), lines)

    def port_mixes(part):
        lines = []
        width = group_dev * N
        lanes = slice(width_dev + part * width, width_dev + (part + 1) * width)
        for position in range(rim_rows):
            old = [old_ports[member, position].astype(F32)[part : part + 1] for member in range(2)]
            lines.append(pick(old[0], old[1], tails[position : position + 1, lanes]))
        lines += [new_ports[index].astype(F32)[:, part, :] for index in range(count)]
        return mix(port_taps[...].astype(F32)[:, part, :], lines)

    writes, read_rows = port_mixes(0), port_mixes(1)
    size = softplus(steps[...])
    log_decay = size * -jnp.exp(log_row[...])
    sizes = [size[index * rows_dev : (index + 1) * rows_dev] for index in range(count)]
    logs = [log_decay[index * rows_dev : (index + 1) * rows_dev] for index in range(count)]
    lane = lax.broadcasted_iota(jnp.int32, (rows_dev, heads), 1)
    per_group = heads // group_dev
    stack, spots = [], {}
    total = None
    starts = []
    for index in range(count):
        total = logs[index] if total is None else total + logs[index]
        starts.append(jnp.exp(total))
    start_all = jnp.concatenate(starts, axis=0)
    kept = jnp.where(chosen, 0.0, start_all)
    given = jnp.where(chosen, start_all, 0.0)
    for index in range(count):
        gap = None
        for earlier in range(index, -1, -1):
            product = read_rows[index] * writes[earlier]
            meets = jnp.zeros((rows_dev, heads), F32)
            for group in range(group_dev):
                met = jnp.sum(product[:, group * N : (group + 1) * N], axis=1, keepdims=True)
                meets = jnp.where(lax.div(lane, per_group) == group, met, meets)
            weight = meets * sizes[earlier]
            if earlier == index:
                weight = weight + skip[...]
            else:
                gap = logs[earlier + 1] if gap is None else gap + logs[earlier + 1]
                weight = weight * jnp.exp(gap)
            spots[index, earlier] = count * rows_dev + len(stack) * rows_dev
            stack.append(weight)
    coefficients = paired(jnp.concatenate([kept] + stack, axis=0))
    shared = paired(given)
    reads = jnp.concatenate(read_rows, axis=0).astype(BF16)
    quarters = width_dev // piece
    per = quarters // group_dev
    for quarter in range(quarters):
        lanes = slice(quarter * piece, (quarter + 1) * piece)
        group = quarter // per
        read = reads[:, group * N : (group + 1) * N]
        wide = dot(coefficients, head_spread(quarter, heads, piece))
        values = value_mixes(lanes)
        met = jnp.where(
            second, dot_nt(read, cache[1, lanes, :]), dot_nt(read, cache[0, lanes, :])
        )
        results = []
        for index in range(count):
            at = index * rows_dev
            line = wide[at : at + rows_dev] * met[at : at + rows_dev]
            for earlier in range(index + 1):
                spot = spots[index, earlier]
                line = line + wide[spot : spot + rows_dev] * values[earlier]
            results.append(line)
        out[quarter, :, 0:piece] = jnp.concatenate(results, axis=0).astype(BF16)
        out[quarter, :, piece : piece + N] = read
        out[quarter, :, piece + N : piece + N + 2 * heads] = shared


def copy_kernel(ids, source, out):
    out[...] = source[...]


def order_kernel(ids, *refs):
    out, done = refs[Y : Y + 2]
    done[...] = jnp.zeros(done.shape, F32)
    for index in range(Y):
        out[wrapped(ids, index)] = refs[index][...]


def project_kernel(ids, back, *refs):
    pieces, blocks = refs[0 : Z * X], refs[Z * X : Z * X + Y]
    keep, send, final, joined = refs[Z * X + Y : Z * X + Y + 4]
    width = joined.shape[1]
    each = back.shape[2]
    rows = pieces[0].shape[0]
    for owner in range(back.shape[0]):
        final[:, owner * each : (owner + 1) * each] = back[owner, N : 2 * N]
    pairs = pieces[0].shape[1] - width - N
    spread = head_spread(ids[2], pairs // 2, width)
    for index in range(X):
        for member in range(Z):
            piece = pieces[member * X + index]
            at = (index * Z + member) * rows
            for start in range(0, width, 256):
                lanes = slice(start, start + 256)
                extra = dot(piece[:, width + N :], spread[:, lanes]) * dot(
                    piece[:, width : width + N], final[:, lanes]
                )
                joined[at : at + rows, lanes] = (piece[:, lanes].astype(F32) + extra).astype(BF16)
    for block in range(Y):
        part = dot(joined[...], blocks[block][...]).astype(BF16)
        for index in range(X):
            spot = lax.rem(ids[0] + index, X)
            same = lax.rem(spot, 2) == ids[3]
            row = lax.div(spot, 2)
            lines = part[index * Z * rows : (index + 1) * Z * rows]

            @pl.when(same)
            def _():
                keep[block, row] = lines

            @pl.when(jnp.logical_not(same))
            def _():
                send[block, row] = lines


def pair_sum_kernel(ids, keep, other, own, *outs):
    own[...] = keep[0].astype(F32) + other[0].astype(F32)
    for index in range(1, Y):
        outs[index - 1][...] = (keep[index].astype(F32) + other[index].astype(F32)).astype(BF16)


def ring_sum_kernel(ids, own, first, second, third, mine, theirs):
    high = ids[4]

    def total(at):
        return (
            own[at] + first[at].astype(F32) + second[at].astype(F32) + third[at].astype(F32)
        )

    mine[...] = total(high)
    theirs[...] = total(1 - high).astype(BF16)


def finish_kernel(ids, mine, other, out):
    total = mine[...] + other[...].astype(F32)
    count = out.shape[0]
    rows = out.shape[1] // (Z * Y)
    for member in range(Z):
        spot = lax.rem(ids[1] + member, Z)
        for index in range(count):
            lines = []
            for turn in range(Y):
                at = ((member * Y + turn) * count + index) * rows
                lines.append(total[at : at + rows])
            out[index, pl.ds(pl.multiple_of(spot * Y * rows, Y * rows), Y * rows), :] = (
                jnp.concatenate(lines, axis=0).astype(BF16)
            )


def shards(
    raw_values,
    state_ports,
    step_raw,
    decay_log,
    skip_gain,
    conv_values,
    conv_ports,
    prompt_slot,
    row_slot,
    cache_states,
    cache_values,
    cache_ports,
    new_values,
    new_ports,
    new_steps,
    out_weight,
):
    length, width_dev = raw_values.shape
    heads = decay_log.shape[0]
    ports_dev = 2 * state_ports.shape[2]
    rim_rows = CONV - 1
    width = width_dev // Y
    count, rows_dev = new_steps.shape[0:2]
    per = Y * N // state_ports.shape[2]
    me = lax.axis_index("ctx").astype(jnp.int32)
    part = lax.axis_index("head").astype(jnp.int32)
    my_x, my_z, my_y = me // (Z * Y), me // Y % Z, me % Y
    my_core, my_high = part % 2, part // 2
    ids = jnp.concatenate(
        [jnp.stack([my_x, my_z, my_y, my_core, my_high]), prompt_slot, row_slot]
    )
    devices = X * Z * Y
    log_row = decay_log.reshape(1, heads)
    skip_row = skip_gain.reshape(1, heads)

    def quarter_block(block, index, dim):
        def at(s, i):
            spot = [0] * len(block)
            spot[dim] = wrapped(s, index)
            return tuple(spot)

        return block, at

    edge = 16
    last_edge = length // edge - 1
    tails = call(
        tails_kernel,
        ids,
        [
            (raw_values, (edge, width_dev), lambda s, i: (last_edge, 0)),
            (state_ports, (edge,) + state_ports.shape[1:], lambda s, i: (last_edge, 0, 0)),
        ],
        [sds((rim_rows, width_dev + ports_dev), BF16)],
    )[0]
    rim = lax.ppermute(tails, "ctx", [(i, i + 1) for i in range(devices - 1)])
    last = devices - 1
    moved = tails
    for step in range(1, Y):
        at_y = lax.ppermute(tails, "ctx", [(last, last - step)])
        moved = jnp.where(my_y == Y - 1 - step, at_y, moved)
    home_y = moved
    at_z = lax.ppermute(
        home_y, "ctx", [(place(X - 1, Z - 1, y), place(X - 1, 0, y)) for y in range(Y)]
    )
    moved = jnp.where(my_z == Z - 1, home_y, at_z)
    homes = [moved]
    for step in range(1, X):
        homes.append(
            lax.ppermute(
                moved,
                "ctx",
                [(place(X - 1, z, y), place(X - 1 - step, z, y)) for z in range(Z) for y in range(Y)],
            )
        )

    span = call(
        span_kernel,
        ids,
        [
            raw_values,
            state_ports.reshape(length, ports_dev),
            rim,
            conv_values,
            conv_ports,
            step_raw.T,
            log_row,
            skip_row,
        ],
        [
            sds((SPAN, ports_dev // 2), BF16),
            sds((ports_dev // 2, SPAN), BF16),
            sds((Y, SPAN, heads // Y), F32),
            sds((heads, SPAN), F32),
            sds((SPAN + 16, 2 * heads), BF16),
            sds((Y, SPAN, width), BF16),
        ]
        + [sds((N + 16, width), BF16)] * Y
        + [sds((8, 128), F32)],
        scratch=[
            pltpu.VMEM((SPAN + 8, width), F32),
            pltpu.VMEM((SPAN + 16, width), F32),
            pltpu.VMEM((SPAN, width), BF16),
        ],
    )
    shared, states, spanned = span[0:6], span[6 : 6 + Y], span[6 + Y]
    ring = [states[0], None, None, None]
    for index in (1, 3, 2):
        ring[Y - index] = shifted(states[index], dy=index)

    packed_width = width + N + 2 * heads
    slots = cache_states.shape[0]
    packed = call(
        decode_kernel,
        ids,
        [
            *homes,
            cache_values.transpose(1, 0, 2),
            cache_ports,
            new_values,
            new_ports,
            conv_values,
            conv_ports,
            new_steps.reshape(count * rows_dev, heads),
            log_row,
            skip_row,
            cache_states.reshape(slots, width_dev, N),
        ],
        [sds((Y, count * rows_dev, packed_width), BF16)],
        after=[spanned],
    )[0]
    quarters = [(my_y + index) % Y for index in range(Y)]
    by_y = [lax.dynamic_index_in_dim(packed, quarters[0], 0, False), None, None, None]
    for index in range(1, Y):
        by_y[Y - index] = shifted(
            lax.dynamic_index_in_dim(packed, quarters[index], 0, False), dy=index
        )
    ordered, turned = call(
        order_kernel,
        ids,
        by_y,
        [sds((Y, count * rows_dev, packed_width), BF16), sds((8, 128), F32)],
    )
    piece_rows = Z * Y * count * rows_dev
    pieces = []
    for held in (ordered, shifted(ordered, dz=1)):
        held = held.reshape(Y * count * rows_dev, packed_width)
        pieces += [held] + [shifted(held, dx=-index) for index in range(1, X)]

    owners = X * Z
    each = width // owners
    groups = [[place(x, z, y) for x in range(X) for z in range(Z)] for y in range(Y)]
    totals, summed = call(
        row_total_kernel,
        ids,
        ring,
        [sds((owners, N + 16, each), BF16), sds((8, 128), F32)],
        after=[turned],
    )
    totals = lax.all_to_all(totals, "ctx", 0, 0, tiled=True, axis_index_groups=groups)
    back = call(chain_kernel, ids, [totals], [sds((owners, 2 * N, each), BF16)])[0]
    back = lax.all_to_all(back, "ctx", 0, 0, tiled=True, axis_index_groups=groups)
    prefixes = call(
        prefix_kernel,
        ids,
        [back, *ring],
        [sds((N, width), BF16) for _ in range(Y)],
    )
    incoming = [prefixes[0], None, None, None]
    for index in (1, 3, 2):
        incoming[Y - index] = shifted(prefixes[index], dy=index)

    def weight_block(index, after=()):
        return call(
            copy_kernel,
            ids,
            [(out_weight, *quarter_block((width, out_weight.shape[1]), index, 0))],
            [sds((width, out_weight.shape[1]), BF16)],
            after=after,
        )[0]

    blocks = [None] * Y
    for index in (1, 3, 2):
        blocks[Y - index] = shifted(weight_block(index, after=[summed]), dy=index)

    cols = out_weight.shape[1]
    keep, send = call(
        project_kernel,
        ids,
        [
            back,
            *pieces,
            (out_weight, *quarter_block((width, cols), 0, 0)),
            *blocks[1:],
        ],
        [sds((Y, X // 2, piece_rows, cols), BF16)] * 2,
        scratch=[pltpu.VMEM((N, width), BF16), pltpu.VMEM((X * piece_rows, width), BF16)],
        after=[incoming[1][0:16, 0:128], incoming[3][0:16, 0:128]],
    )
    other = lax.ppermute(send, "head", [(i, i ^ 1) for i in range(4)])
    half = (X // 2, piece_rows, cols)
    own, *outward = call(
        pair_sum_kernel,
        ids,
        [keep, other],
        [sds(half, F32)] + [sds(half, BF16)] * (Y - 1),
    )
    inward = [shifted(outward[index - 1], dy=index) for index in (1, 3, 2)]
    mine, theirs = call(
        ring_sum_kernel, ids, [own, *inward], [sds(half[1:], F32), sds(half[1:], BF16)]
    )
    other = lax.ppermute(theirs, "head", [(i, i ^ 2) for i in range(4)])
    decoded_out = call(
        finish_kernel, ids, [mine, other], [sds((count, Z * Y * rows_dev, cols), BF16)]
    )[0]

    def turn_block(indices):
        def at(s, i):
            index = indices[0]
            for turn in range(1, len(indices)):
                index = jnp.where(i == turn, indices[turn], index)
            return 0, wrapped(s, index)

        return at

    scan_out = None
    for indices in ((0, 1, 3), (2,)):
        scan_out = call(
            functools.partial(scan_kernel, indices),
            ids,
            [*shared, *[incoming[index] for index in indices]],
            [(sds((SPAN, width_dev), BF16), (SPAN, width), turn_block(indices))],
            scratch=[pltpu.VMEM((SPAN, SPAN), F32), pltpu.VMEM((SPAN + 16, width), F32)],
            into=scan_out,
            turns=len(indices),
        )[0]
    return scan_out, decoded_out


def solution(mesh):
    in_specs = (
        P("ctx", "head"),
        P("ctx", None, "head"),
        P("ctx", "head"),
        P("head"),
        P("head"),
        P(None, "head"),
        P(None, None, "head"),
        P("ctx"),
        P("ctx"),
        P("ctx", "head", None, None),
        P("ctx", None, "head"),
        P("ctx", None, None, "head"),
        P(None, "ctx", "head"),
        P(None, "ctx", None, "head"),
        P(None, "ctx", "head"),
        P("head", "ctx"),
    )
    out_specs = (P("ctx", "head"), P(None, "head", "ctx"))
    return jax.shard_map(shards, mesh=mesh, in_specs=in_specs, out_specs=out_specs, check_vma=False)
```
